32 devices in a mesh: px: 4 (over y, core), py: 8 (over z, x).
Axes of the slice: x: 2, y: 2, z: 4, core: 2. Of those that a mesh axis runs over, the one named last changes fastest.
Arguments:
- kappa: bfloat16 [76800, 128], P(('px', 'py')), may hold values from -6 to 6
- send_list: int32 [32, 32, 384], P(('px', 'py')), may hold values from 0 to 2399, as said below
- dest_slot: int32 [32, 32, 384], P(('px', 'py')), may hold values from 0 to 2047, as said below
- send_count: int32 [32, 32], P(('px', 'py')), may hold values from 0 to 384, as said below
Outputs:
- flexion: float32 [4, 2048, 4096], P(None, 'px', 'py')
The draws below stay inside these ranges and needn't reach their ends.
Inputs may be any that keep to these rules, and one draw needn't show every extreme that they name: For k < send_count[a, d], send_list[a, d, k] is a row of source a's own 2400 tiles; later entries are 0. Over all sources a and k < send_count[a, d], dest_slot[a, d, k] names every slot of patch d exactly once; later entries are 0. send_count[a, d] is nonzero only where d's patch row equals a's px index or is one less; it is a multiple of 4, and reaches 384 in every draw. Summed over the sources a whose px index is one more than d's patch row, it is exactly 512.
All inputs are finite; a program needn't handle non-finite values.
Results may differ from the reference program's by a relative error of at most 0.0065.
Values may be sent and summed in bfloat16 or wider, within the bound.
A program may use at most 64 MiB of HBM per device.

```python
import math
import jax
import jax.numpy as jnp
from jax import lax

PATCH_ROWS = 512
PATCH_COLS = 512
TILE = 128
TILES_ROW = 4
SLOTS = 2048
BAND_ROWS = 384
CYCLE_TILES = 25
CYCLE_MOST = 96
TILE_DEV = 2400
CAP = 384
N_PX = 4
N_PY = 8


def band_lengths(key):
    collected = []
    for band_number in range(N_PX):
        total_rows = PATCH_ROWS if band_number == N_PX - 1 else BAND_ROWS
        extra_units = total_rows - CYCLE_MOST - (N_PY - 1)
        band_key = jax.random.fold_in(key, 1000 + band_number)
        first_key, second_key = jax.random.split(band_key)
        busiest = jax.random.randint(first_key, (), 0, N_PY)
        unit_order = jax.random.permutation(second_key, (N_PY - 1) * (CYCLE_MOST - 1))
        chosen = (unit_order < extra_units).astype(jnp.int32).reshape(N_PY - 1, CYCLE_MOST - 1)
        others = 1 + jnp.sum(chosen, axis=1)
        places = jnp.arange(N_PY, dtype=jnp.int32)
        shifted = jnp.clip(places - (places > busiest).astype(jnp.int32), 0, N_PY - 2)
        collected.append(jnp.where(places == busiest, CYCLE_MOST, others[shifted]))
    return jnp.stack(collected).astype(jnp.int32)


def routing(key):
    lengths = band_lengths(jax.random.fold_in(key, 77))
    starts = jnp.cumsum(lengths, axis=1) - lengths
    src_band = jnp.arange(N_PX, dtype=jnp.int32)[:, None, None, None, None]
    dst_band = jnp.arange(N_PX, dtype=jnp.int32)[None, None, :, None, None]
    dst_col = jnp.arange(N_PY, dtype=jnp.int32)[None, None, None, :, None]
    slot_pos = jnp.arange(CAP, dtype=jnp.int32)[None, None, None, None, :]
    length = lengths[:, :, None, None, None]
    start = starts[:, :, None, None, None]
    same_row = dst_band == src_band
    row_above = dst_band == src_band - 1
    rise_count = jnp.clip(jnp.minimum(start + length, TILE) - start, 0, None) * TILES_ROW
    count = jnp.where(same_row, length * TILES_ROW, jnp.where(row_above, rise_count, 0))
    count = jnp.broadcast_to(count, (N_PX, N_PY, N_PX, N_PY, 1))
    band_local = slot_pos // TILES_ROW
    column = slot_pos % TILES_ROW
    band_row = start + band_local
    local_row = band_local * CYCLE_TILES + dst_col * (TILES_ROW - 1) + column
    patch_row = jnp.where(same_row, band_row, band_row + BAND_ROWS)
    slot_value = patch_row * TILES_ROW + column
    live_mask = slot_pos < count
    devices = N_PX * N_PY
    lists = jnp.where(live_mask, local_row, 0).astype(jnp.int32).reshape(devices, devices, CAP)
    slots = jnp.where(live_mask, slot_value, 0).astype(jnp.int32).reshape(devices, devices, CAP)
    counts = count[..., 0].astype(jnp.int32).reshape(devices, devices)
    return (lists, slots, counts)


def draw_send_list(key, part):
    return routing(key)[0]


def draw_dest_slot(key, part):
    return routing(key)[1]


def draw_send_count(key, part):
    return routing(key)[2]


def level_of(stream_key, extent, cuts, low, top_value):
    factor_of = 1.0
    for dim, blocks in cuts:
        heights = jax.random.uniform(jax.random.fold_in(jax.random.fold_in(stream_key, 6), dim), (blocks,), jnp.float32, low / len(cuts), top_value / len(cuts))
        factor_of = factor_of * jnp.repeat(jnp.exp(heights), extent[dim] // blocks).reshape((-1,) + (1,) * (len(extent) - 1 - dim))
    return factor_of


def bell_draw(key, extent, scale, reach, shards=(), kind=jnp.bfloat16):
    values = jax.random.normal(key, extent, jnp.float32) * scale
    if len(shards) > 0:
        values = level_of(key, extent, shards, -0.22, 0.18) * values
    return jnp.clip(values, min=-reach, max=reach).astype(kind)


def setup_inputs(seed: int = 0) -> dict:
    key_of = jax.random.split(jax.random.key(seed), 5)
    kappa = bell_draw(key_of[0], (N_PX * N_PY * TILE_DEV, TILE), 1.0, 6.0, ((0, 32),))
    send_list = draw_send_list(jax.random.fold_in(key_of[4], 71), 0)
    dest_slot = draw_dest_slot(jax.random.fold_in(key_of[4], 71), 0)
    send_count = draw_send_count(jax.random.fold_in(key_of[4], 71), 0)
    return dict(kappa=kappa, send_list=send_list, dest_slot=dest_slot, send_count=send_count)


def dft_tables(length):
    positions = jnp.arange(length, dtype=jnp.int32)
    phases = (positions[:, None] * positions[None, :]) % length
    angles = phases.astype(jnp.float32) * (2.0 * math.pi / length)
    return jnp.cos(angles), jnp.sin(angles)


def wavenumbers(length):
    positions = jnp.arange(length, dtype=jnp.int32)
    signed = positions - length * (positions >= (length + 1) // 2).astype(jnp.int32)
    return signed.astype(jnp.float32) * (2.0 / length)


def flexion_fields(pixels):
    row_count = pixels.shape[0]
    col_count = pixels.shape[1]
    cos_cols, sin_cols = dft_tables(col_count)
    cos_rows, sin_rows = dft_tables(row_count)
    forward_cols = jnp.concatenate([cos_cols, sin_cols], axis=1).astype(jnp.bfloat16)
    halves = jnp.dot(pixels, forward_cols, preferred_element_type=jnp.float32)
    stacked = jnp.concatenate([halves[:, :col_count], halves[:, col_count:]], axis=0).astype(jnp.bfloat16)
    forward_rows = jnp.concatenate([jnp.concatenate([cos_rows, -sin_rows], axis=1), jnp.concatenate([-sin_rows, -cos_rows], axis=1)], axis=0).astype(jnp.bfloat16)
    spectrum = jnp.dot(forward_rows, stacked, preferred_element_type=jnp.float32)
    real_part = spectrum[:row_count]
    imag_part = spectrum[row_count:]
    across = wavenumbers(col_count)[None, :]
    down = wavenumbers(row_count)[:, None]
    scale = 1.0 / (row_count * col_count)
    power = across * across + down * down
    safe_power = jnp.where(power > 0, power, 1.0)
    cube_real = across * across * across - 3.0 * across * down * down
    cube_imag = 3.0 * across * across * down - down * down * down
    one_real = (-down * real_part - across * imag_part) * scale
    one_imag = (across * real_part - down * imag_part) * scale
    kernel_real = -cube_imag / safe_power
    kernel_imag = cube_real / safe_power
    three_real = (kernel_real * real_part - kernel_imag * imag_part) * scale
    three_imag = (kernel_real * imag_part + kernel_imag * real_part) * scale
    spectra = jnp.concatenate([jnp.concatenate([one_real, three_real], axis=1), jnp.concatenate([one_imag, three_imag], axis=1)], axis=0).astype(jnp.bfloat16)
    inverse_rows = jnp.concatenate([jnp.concatenate([cos_rows, -sin_rows], axis=1), jnp.concatenate([sin_rows, cos_rows], axis=1)], axis=0).astype(jnp.bfloat16)
    columns_done = jnp.dot(inverse_rows, spectra, preferred_element_type=jnp.float32).astype(jnp.bfloat16)
    arranged = jnp.concatenate([
        jnp.concatenate([columns_done[:row_count, :col_count], columns_done[row_count:, :col_count]], axis=1),
        jnp.concatenate([columns_done[:row_count, col_count:], columns_done[row_count:, col_count:]], axis=1)], axis=0)
    inverse_cols = jnp.concatenate([jnp.concatenate([cos_cols, sin_cols], axis=1), jnp.concatenate([-sin_cols, cos_cols], axis=1)], axis=0).astype(jnp.bfloat16)
    result = jnp.dot(arranged, inverse_cols, preferred_element_type=jnp.float32)
    return jnp.stack([result[:row_count, :col_count], result[:row_count, col_count:], result[row_count:, :col_count], result[row_count:, col_count:]]).astype(jnp.bfloat16)


def blend_edges(extended, has_top, has_bottom, has_left, has_right, width):
    values = extended.astype(jnp.float32)
    row_count = values.shape[1] - 2 * width
    col_count = values.shape[2] - 2 * width
    ramp = (jnp.arange(width, dtype=jnp.float32) + 0.5) / width
    top_weight = jnp.where(has_top, ramp, 1.0)[None, :, None]
    bottom_weight = jnp.where(has_bottom, ramp[::-1], 1.0)[None, :, None]
    middle = values[:, width:width + row_count, :]
    top_band = top_weight * middle[:, :width] + (1.0 - top_weight) * values[:, :width]
    bottom_band = bottom_weight * middle[:, row_count - width:] + (1.0 - bottom_weight) * values[:, row_count + width:]
    middle = jnp.concatenate([top_band, middle[:, width:row_count - width], bottom_band], axis=1)
    left_weight = jnp.where(has_left, ramp, 1.0)[None, None, :]
    right_weight = jnp.where(has_right, ramp[::-1], 1.0)[None, None, :]
    inner = middle[:, :, width:width + col_count]
    left_band = left_weight * inner[:, :, :width] + (1.0 - left_weight) * middle[:, :, :width]
    right_band = right_weight * inner[:, :, col_count - width:] + (1.0 - right_weight) * middle[:, :, col_count + width:]
    return jnp.concatenate([left_band, inner[:, :, width:col_count - width], right_band], axis=2)


def reference(kappa, send_list, dest_slot, send_count):
    devices = N_PX * N_PY
    tile_width = kappa.shape[1]
    tile_table = kappa.reshape(devices, TILE_DEV, tile_width)
    sources = jnp.arange(devices, dtype=jnp.int32)[:, None]
    slot_depth = jnp.arange(CAP, dtype=jnp.int32)[None, :]

    def one_patch(patch_number):
        chosen = send_list[:, patch_number, :]
        tile_values = tile_table[sources, chosen]
        live_mask = slot_depth < send_count[:, patch_number][:, None]
        target = jnp.where(live_mask, dest_slot[:, patch_number, :], SLOTS)
        patch_tiles = jnp.zeros((SLOTS, tile_width), kappa.dtype).at[target.reshape(-1)].set(tile_values.reshape(-1, tile_width), mode="drop")
        return flexion_fields(patch_tiles.reshape(PATCH_ROWS, PATCH_COLS))

    numbers = jnp.arange(devices, dtype=jnp.int32)
    fields = lax.map(one_patch, numbers)
    field_grid = fields.reshape(N_PX, N_PY, 4, PATCH_ROWS, PATCH_COLS)
    padded = jnp.pad(field_grid, ((1, 1), (1, 1), (0, 0), (0, 0), (0, 0)))

    def one_blend(patch_number):
        band_index = patch_number // N_PY
        column_index = patch_number % N_PY
        zero_index = jnp.zeros((), jnp.int32)
        neighbours = lax.dynamic_slice(padded, (band_index, column_index, zero_index, zero_index, zero_index), (3, 3, 4, PATCH_ROWS, PATCH_COLS))
        stacks = []
        for offset in range(3):
            stacks.append(jnp.concatenate([neighbours[0, offset, :, PATCH_ROWS - TILE:], neighbours[1, offset], neighbours[2, offset, :, :TILE]], axis=1))
        extended = jnp.concatenate([stacks[0][:, :, PATCH_COLS - TILE:], stacks[1], stacks[2][:, :, :TILE]], axis=2)
        return blend_edges(extended, band_index > 0, band_index < N_PX - 1, column_index > 0, column_index < N_PY - 1, TILE)

    blended = lax.map(one_blend, numbers)
    blended = blended.reshape(N_PX, N_PY, 4, PATCH_ROWS, PATCH_COLS).transpose(2, 0, 3, 1, 4)
    return blended.reshape(4, N_PX * PATCH_ROWS, N_PY * PATCH_COLS)
```

```python
import functools
import math

import jax
import jax.numpy as jnp
import numpy as np
from jax import lax
from jax.experimental import pallas as pl
from jax.experimental.pallas import tpu as pltpu
from jax.sharding import PartitionSpec as P

PATCH = 512
MESH = pl.DeviceIdType.MESH
STEP = 16


def gather_kernel(n_px, n_py, kappa_ref, list_ref, count_ref, slot_ref, tiles_ref, aux_ref, wide, stage):
    i = lax.axis_index("px")
    j = lax.axis_index("py")
    cap = list_ref.shape[2]
    width = aux_ref.shape[3]
    wide[...] = kappa_ref[...].astype(jnp.float32)
    lanes = lax.broadcasted_iota(jnp.int32, (1, cap), 1)
    dump = PATCH * PATCH // kappa_ref.shape[1]

    def one(t, carry):
        b = t // n_py
        o = lax.rem(t, n_py)
        row = jnp.maximum(i - b, 0)
        d = row * n_py + lax.rem(j + o, n_py)
        count = jnp.where(i - b >= 0, count_ref[0, d], 0)

        def rows(c, carry):
            base = pl.multiple_of(c * STEP, STEP)
            for k in range(STEP):
                source = list_ref[0, d, base + k]
                stage[pl.ds(base + k, 1), :] = wide[pl.ds(source, 1), :]
            return carry

        lax.fori_loop(0, (count + STEP - 1) // STEP, rows, 0)
        tiles_ref[b, o] = stage[...].astype(jnp.bfloat16)
        slots = slot_ref[0, pl.ds(d, 1), :]
        aux_ref[b, o] = jnp.full((1, width), count, jnp.int32)
        aux_ref[b, o, :, :cap] = jnp.where(lanes < count, slots, dump)
        return carry

    lax.fori_loop(0, 2 * n_py, one, 0)


def gather_tiles(n_px, n_py, kappa, send_list, dest_slot, send_count):
    cap = send_list.shape[2]
    width = (cap + 128) // 128 * 128
    vmem = pl.BlockSpec(memory_space=pltpu.VMEM)
    smem = pl.BlockSpec(memory_space=pltpu.SMEM)
    return pl.pallas_call(
        functools.partial(gather_kernel, n_px, n_py),
        out_shape=(
            jax.ShapeDtypeStruct((2, n_py, cap, kappa.shape[1]), jnp.bfloat16),
            jax.ShapeDtypeStruct((2, n_py, 1, width), jnp.int32),
        ),
        in_specs=[vmem, smem, smem, vmem],
        out_specs=(vmem, vmem),
        scratch_shapes=[
            pltpu.VMEM(kappa.shape, jnp.float32),
            pltpu.VMEM((cap, kappa.shape[1]), jnp.float32),
        ],
        compiler_params=pltpu.CompilerParams(vmem_limit_bytes=32 * 2**20),
        name="gather_tiles",
    )(kappa, send_list, send_count, dest_slot)


def exchange_kernel(n_px, n_py, tiles, aux, got_tiles, got_aux, send_t, recv_t, send_a, recv_a, local):
    i = lax.axis_index("px")
    j = lax.axis_index("py")
    has_up = i > 0
    has_down = i < n_px - 1
    barrier = pltpu.get_barrier_semaphore()
    for o in range(1, n_py):
        pl.semaphore_signal(barrier, inc=1, device_id=(i, lax.rem(j + o, n_py)), device_id_type=MESH)

    @pl.when(has_down)
    def _():
        for o in range(n_py):
            pl.semaphore_signal(
                barrier, inc=1, device_id=(i + 1, lax.rem(j + o, n_py)), device_id_type=MESH
            )

    pl.semaphore_wait(barrier, n_py - 1 + jnp.where(has_up, n_py, 0))

    def copies(b, o):
        target = (i - b, lax.rem(j + o, n_py))
        return [
            pltpu.make_async_remote_copy(
                src_ref=source.at[b, o],
                dst_ref=landing.at[b, o],
                send_sem=send.at[b, o],
                recv_sem=recv.at[b, o],
                device_id=target,
                device_id_type=MESH,
            )
            for source, landing, send, recv in (
                (tiles, got_tiles, send_t, recv_t),
                (aux, got_aux, send_a, recv_a),
            )
        ]

    own = [
        pltpu.make_async_copy(tiles.at[0, 0], got_tiles.at[0, 0], local.at[0]),
        pltpu.make_async_copy(aux.at[0, 0], got_aux.at[0, 0], local.at[1]),
    ]
    for copy in own:
        copy.start()
    order = sorted(range(n_py), key=lambda o: -min(o, n_py - o))
    for o in order:
        if o > 0:
            for copy in copies(0, o):
                copy.start()

        @pl.when(has_up)
        def _():
            for copy in copies(1, o):
                copy.start()

    for o in order:
        if o > 0:
            for copy in copies(0, o):
                copy.wait()

        @pl.when(has_up)
        def _():
            for copy in copies(1, o):
                copy.wait_send()

        @pl.when(has_down)
        def _():
            for copy in copies(1, o):
                copy.wait_recv()

    for copy in own:
        copy.wait()


def exchange(n_px, n_py, tiles, aux):
    anywhere = pl.BlockSpec(memory_space=pl.ANY)
    return pl.pallas_call(
        functools.partial(exchange_kernel, n_px, n_py),
        out_shape=(
            jax.ShapeDtypeStruct(tiles.shape, tiles.dtype),
            jax.ShapeDtypeStruct(aux.shape, aux.dtype),
        ),
        in_specs=[anywhere] * 2,
        out_specs=(anywhere, anywhere),
        scratch_shapes=[pltpu.SemaphoreType.DMA((2, n_py))] * 4 + [pltpu.SemaphoreType.DMA((2,))],
        compiler_params=pltpu.CompilerParams(collective_id=0, has_side_effects=True),
        name="exchange_tiles",
    )(tiles, aux)


def place_kernel(n_px, n_py, tiles_ref, aux_ref, image_ref, wide, patch):
    i = lax.axis_index("px")
    cap = tiles_ref.shape[2]
    per_row = PATCH // tiles_ref.shape[3]
    tile = tiles_ref.shape[3]

    def one(t, carry):
        b = t // n_py
        o = lax.rem(t, n_py)
        live = jnp.logical_or(b == 0, i < n_px - 1)

        @pl.when(live)
        def _():
            wide[...] = tiles_ref[b, o].astype(jnp.float32)

            def rows(c, carry):
                base = pl.multiple_of(c * STEP, STEP)
                for k in range(STEP):
                    slot = aux_ref[b, o, 0, base + k]
                    patch[pl.ds(slot, 1), :] = wide[pl.ds(base + k, 1), :]
                return carry

            lax.fori_loop(0, (aux_ref[b, o, 0, cap] + STEP - 1) // STEP, rows, 0)

        return carry

    lax.fori_loop(0, 2 * n_py, one, 0)
    for c in range(per_row):
        image_ref[:, c * tile : (c + 1) * tile] = patch[
            pl.ds(c, PATCH, stride=per_row), :
        ].astype(jnp.bfloat16)


def place_tiles(n_px, n_py, tiles, aux):
    vmem = pl.BlockSpec(memory_space=pltpu.VMEM)
    smem = pl.BlockSpec(memory_space=pltpu.SMEM)
    tile = tiles.shape[3]
    return pl.pallas_call(
        functools.partial(place_kernel, n_px, n_py),
        out_shape=jax.ShapeDtypeStruct((PATCH, PATCH), jnp.bfloat16),
        in_specs=[vmem, smem],
        out_specs=vmem,
        scratch_shapes=[
            pltpu.VMEM((tiles.shape[2], tile), jnp.float32),
            pltpu.VMEM((PATCH * PATCH // tile + 8, tile), jnp.float32),
        ],
        compiler_params=pltpu.CompilerParams(vmem_limit_bytes=32 * 2**20),
        name="place_tiles",
    )(tiles, aux)


def dft_tables(length):
    positions = np.arange(length)
    angles = (positions[:, None] * positions[None, :] % length).astype(np.float32) * np.float32(
        2.0 * math.pi / length
    )
    return np.cos(angles).astype(np.float32), np.sin(angles).astype(np.float32)


def wavenumbers(length):
    positions = np.arange(length)
    return (positions - length * (positions >= (length + 1) // 2)).astype(np.float32) * np.float32(2.0 / length)


def flexion_fields(pixels):
    n = pixels.shape[0]
    cos, sin = dft_tables(n)
    bf16 = jnp.bfloat16
    halves = jnp.dot(pixels, jnp.asarray(np.concatenate([cos, sin], 1), bf16), preferred_element_type=jnp.float32)
    stacked = jnp.concatenate([halves[:, :n], halves[:, n:]], axis=0).astype(bf16)
    forward = np.block([[cos, -sin], [-sin, -cos]])
    spectrum = jnp.dot(jnp.asarray(forward, bf16), stacked, preferred_element_type=jnp.float32)
    real_part, imag_part = spectrum[:n], spectrum[n:]
    across = wavenumbers(n)[None, :]
    down = wavenumbers(n)[:, None]
    scale = np.float32(1.0 / (n * n))
    power = across * across + down * down
    safe = np.where(power > 0, power, 1.0).astype(np.float32)
    kernel_real = jnp.asarray(-(3.0 * across * across * down - down * down * down) / safe, jnp.float32)
    kernel_imag = jnp.asarray((across * across * across - 3.0 * across * down * down) / safe, jnp.float32)
    across, down = jnp.asarray(across), jnp.asarray(down)
    one_real = (-down * real_part - across * imag_part) * scale
    one_imag = (across * real_part - down * imag_part) * scale
    three_real = (kernel_real * real_part - kernel_imag * imag_part) * scale
    three_imag = (kernel_real * imag_part + kernel_imag * real_part) * scale
    spectra = jnp.concatenate(
        [jnp.concatenate([one_real, three_real], 1), jnp.concatenate([one_imag, three_imag], 1)], 0
    ).astype(bf16)
    inverse = np.block([[cos, -sin], [sin, cos]])
    done = jnp.dot(jnp.asarray(inverse, bf16), spectra, preferred_element_type=jnp.float32).astype(bf16)
    arranged = jnp.concatenate(
        [
            jnp.concatenate([done[:n, :n], done[n:, :n]], 1),
            jnp.concatenate([done[:n, n:], done[n:, n:]], 1),
        ],
        0,
    )
    inverse_cols = np.block([[cos, sin], [-sin, cos]])
    result = jnp.dot(arranged, jnp.asarray(inverse_cols, bf16), preferred_element_type=jnp.float32)
    return jnp.stack([result[:n, :n], result[:n, n:], result[n:, :n], result[n:, n:]]).astype(bf16)


def neighbours(low, high, axis):
    count = lax.axis_size(axis)
    forward = [(k, k + 1) for k in range(count - 1)]
    backward = [(k + 1, k) for k in range(count - 1)]
    return lax.ppermute(high, axis, forward), lax.ppermute(low, axis, backward)


def blend_axis(values, axis, dim, width):
    size = values.shape[dim]
    index = lax.axis_index(axis)
    ramp = (np.arange(width, dtype=np.float32) + np.float32(0.5)) / np.float32(width)
    shape = [1, 1, 1]
    shape[dim] = width
    first = jnp.where(index > 0, ramp, 1.0).reshape(shape)
    last = jnp.where(index < lax.axis_size(axis) - 1, ramp[::-1], 1.0).reshape(shape)
    low = lax.slice_in_dim(values, 0, width, axis=dim)
    high = lax.slice_in_dim(values, size - width, size, axis=dim)
    before, after = neighbours(low.astype(jnp.bfloat16), high.astype(jnp.bfloat16), axis)
    low = first * low.astype(jnp.float32) + (1.0 - first) * before.astype(jnp.float32)
    high = last * high.astype(jnp.float32) + (1.0 - last) * after.astype(jnp.float32)
    middle = lax.slice_in_dim(values, width, size - width, axis=dim).astype(jnp.float32)
    return jnp.concatenate([low, middle, high], axis=dim)


def on_device(kappa, send_list, dest_slot, send_count):
    n_px = lax.axis_size("px")
    n_py = lax.axis_size("py")
    tiles, aux = gather_tiles(n_px, n_py, kappa, send_list, dest_slot, send_count)
    tiles, aux = exchange(n_px, n_py, tiles, aux)
    pixels = place_tiles(n_px, n_py, tiles, aux)
    fields = flexion_fields(pixels)
    rows = blend_axis(fields, "px", 1, kappa.shape[1])
    return blend_axis(rows, "py", 2, kappa.shape[1])


def solution(mesh):
    placed = (
        P(("px", "py"), None),
        P(("px", "py"), None, None),
        P(("px", "py"), None, None),
        P(("px", "py"), None),
    )
    return jax.shard_map(
        on_device, mesh=mesh, in_specs=placed, out_specs=P(None, "px", "py"), check_vma=False
    )
```

```python
import functools
import math

import jax
import jax.numpy as jnp
import numpy as np
from jax import lax
from jax.experimental import pallas as pl
from jax.experimental.pallas import tpu as pltpu
from jax.sharding import PartitionSpec as P

PATCH = 512
MESH = pl.DeviceIdType.MESH
STEP = 16


def gather_kernel(n_px, n_py, kappa_ref, list_ref, count_ref, slot_ref, tiles_ref, aux_ref, wide, stage):
    i = lax.axis_index("px")
    j = lax.axis_index("py")
    cap = list_ref.shape[2]
    width = aux_ref.shape[3]
    wide[...] = kappa_ref[...].astype(jnp.float32)
    lanes = lax.broadcasted_iota(jnp.int32, (1, cap), 1)
    dump = PATCH * PATCH // kappa_ref.shape[1]

    def one(t, carry):
        b = t // n_py
        o = lax.rem(t, n_py)
        row = jnp.maximum(i - b, 0)
        d = row * n_py + lax.rem(j + o, n_py)
        count = jnp.where(i - b >= 0, count_ref[0, d], 0)

        def rows(c, carry):
            base = pl.multiple_of(c * STEP, STEP)
            sources = [list_ref[0, d, base + k] for k in range(STEP)]
            values = [wide[pl.ds(source, 1), :] for source in sources]
            for k in range(STEP):
                stage[pl.ds(base + k, 1), :] = values[k]
            return carry

        lax.fori_loop(0, (count + STEP - 1) // STEP, rows, 0)
        tiles_ref[b, o] = stage[...].astype(jnp.bfloat16)
        slots = slot_ref[0, pl.ds(d, 1), :]
        aux_ref[b, o] = jnp.full((1, width), count, jnp.int32)
        aux_ref[b, o, :, :cap] = jnp.where(lanes < count, slots, dump)
        return carry

    lax.fori_loop(0, 2 * n_py, one, 0)


def gather_tiles(n_px, n_py, kappa, send_list, dest_slot, send_count):
    cap = send_list.shape[2]
    width = (cap + 128) // 128 * 128
    vmem = pl.BlockSpec(memory_space=pltpu.VMEM)
    smem = pl.BlockSpec(memory_space=pltpu.SMEM)
    return pl.pallas_call(
        functools.partial(gather_kernel, n_px, n_py),
        out_shape=(
            jax.ShapeDtypeStruct((2, n_py, cap, kappa.shape[1]), jnp.bfloat16),
            jax.ShapeDtypeStruct((2, n_py, 1, width), jnp.int32),
        ),
        in_specs=[vmem, smem, smem, vmem],
        out_specs=(vmem, vmem),
        scratch_shapes=[
            pltpu.VMEM(kappa.shape, jnp.float32),
            pltpu.VMEM((cap, kappa.shape[1]), jnp.float32),
        ],
        compiler_params=pltpu.CompilerParams(vmem_limit_bytes=32 * 2**20),
        name="gather_tiles",
    )(kappa, send_list, send_count, dest_slot)


def exchange_kernel(n_px, n_py, tiles, aux, got_tiles, got_aux, send_t, recv_t, send_a, recv_a, local):
    i = lax.axis_index("px")
    j = lax.axis_index("py")
    has_up = i > 0
    has_down = i < n_px - 1
    barrier = pltpu.get_barrier_semaphore()
    for o in range(1, n_py):
        pl.semaphore_signal(barrier, inc=1, device_id=(i, lax.rem(j + o, n_py)), device_id_type=MESH)

    @pl.when(has_down)
    def _():
        for o in range(n_py):
            pl.semaphore_signal(
                barrier, inc=1, device_id=(i + 1, lax.rem(j + o, n_py)), device_id_type=MESH
            )

    pl.semaphore_wait(barrier, n_py - 1 + jnp.where(has_up, n_py, 0))

    def copies(b, o):
        target = (i - b, lax.rem(j + o, n_py))
        return [
            pltpu.make_async_remote_copy(
                src_ref=source.at[b, o],
                dst_ref=landing.at[b, o],
                send_sem=send.at[b, o],
                recv_sem=recv.at[b, o],
                device_id=target,
                device_id_type=MESH,
            )
            for source, landing, send, recv in (
                (tiles, got_tiles, send_t, recv_t),
                (aux, got_aux, send_a, recv_a),
            )
        ]

    own = [
        pltpu.make_async_copy(tiles.at[0, 0], got_tiles.at[0, 0], local.at[0]),
        pltpu.make_async_copy(aux.at[0, 0], got_aux.at[0, 0], local.at[1]),
    ]
    for copy in own:
        copy.start()
    order = sorted(range(n_py), key=lambda o: -min(o, n_py - o))
    for o in order:
        if o > 0:
            for copy in copies(0, o):
                copy.start()

        @pl.when(has_up)
        def _():
            for copy in copies(1, o):
                copy.start()

    for o in order:
        if o > 0:
            for copy in copies(0, o):
                copy.wait()

        @pl.when(has_up)
        def _():
            for copy in copies(1, o):
                copy.wait_send()

        @pl.when(has_down)
        def _():
            for copy in copies(1, o):
                copy.wait_recv()

    for copy in own:
        copy.wait()


def exchange(n_px, n_py, tiles, aux):
    anywhere = pl.BlockSpec(memory_space=pl.ANY)
    return pl.pallas_call(
        functools.partial(exchange_kernel, n_px, n_py),
        out_shape=(
            jax.ShapeDtypeStruct(tiles.shape, tiles.dtype),
            jax.ShapeDtypeStruct(aux.shape, aux.dtype),
        ),
        in_specs=[anywhere] * 2,
        out_specs=(anywhere, anywhere),
        scratch_shapes=[pltpu.SemaphoreType.DMA((2, n_py))] * 4 + [pltpu.SemaphoreType.DMA((2,))],
        compiler_params=pltpu.CompilerParams(collective_id=0, has_side_effects=True),
        name="exchange_tiles",
    )(tiles, aux)


def dft_tables(length):
    positions = np.arange(length)
    angles = (positions[:, None] * positions[None, :] % length).astype(np.float32) * np.float32(
        2.0 * math.pi / length
    )
    return np.cos(angles).astype(np.float32), np.sin(angles).astype(np.float32)


def wavenumbers(length):
    positions = np.arange(length)
    return (positions - length * (positions >= (length + 1) // 2)).astype(np.float32) * np.float32(2.0 / length)


def transform_tables(n):
    h = n // 2
    cos, sin = dft_tables(n)
    forward = np.concatenate([cos[:, :h], sin[:, :h]], 1)
    forward[:, h] = cos[:, h]
    down = np.concatenate([cos, sin], 0)
    back_rows = np.block([[cos, -sin], [sin, cos]])
    back_cols = np.concatenate([2.0 * cos[:h], -2.0 * sin[:h]], 0)
    back_cols[0] = 1.0
    back_cols[h] = cos[h]
    signed = wavenumbers(n).astype(np.float64)
    order = np.arange(1, h)
    lag = np.arange(n)
    wave = -(2.0 / n) * (signed[1:h] * np.sin(2.0 * np.pi * (lag[:, None] * order % n) / n)).sum(1)
    slope = wave[(lag[None, :] - lag[:, None]) % n]
    across, along = signed[None, :], signed[:, None]
    power = across**2 + along**2
    lens = 1j * (across + 1j * along) ** 3 / np.where(power > 0, power, 1.0) / (n * n)
    mirror = np.conj(lens[-lag % n][:, -lag % n])
    even, odd = (lens + mirror) / 2, (lens - mirror) / 2j
    weights = np.stack([even.real, even.imag, odd.real, odd.imag])
    edge = np.zeros((4, n, 128))
    edge[:, :, 0] = weights[:, :, h]
    bf16 = [jnp.asarray(t, jnp.bfloat16) for t in (forward, down, back_rows, back_cols, slope)]
    return *bf16, jnp.asarray(weights[:, :, :h], jnp.float32), jnp.asarray(edge, jnp.float32)


def blocked_dot(rows, left, right, write, block=256):
    def one(t, carry):
        start = pl.multiple_of(t * block, block)
        write(start, jnp.dot(left[pl.ds(start, block), :], right[...], preferred_element_type=jnp.float32))
        return carry

    lax.fori_loop(0, rows // block, one, 0)


def fields_kernel(
    n_px, n_py, tiles_ref, aux_ref, forward, down, back_rows, back_cols, slope, weights, edge,
    fields, wide, patch, image, halves, spectrum, spectra, columns,
):
    i = lax.axis_index("px")
    cap = tiles_ref.shape[2]
    tile = tiles_ref.shape[3]
    per_row = PATCH // tile
    n, h = PATCH, PATCH // 2
    bf16, f32 = jnp.bfloat16, jnp.float32

    def one(t, carry):
        b = t // n_py
        o = lax.rem(t, n_py)
        live = jnp.logical_or(b == 0, i < n_px - 1)

        @pl.when(live)
        def _():
            wide[...] = tiles_ref[b, o].astype(f32)

            def rows(c, carry):
                base = pl.multiple_of(c * STEP, STEP)
                slots = [aux_ref[b, o, 0, base + k] for k in range(STEP)]
                values = [wide[pl.ds(base + k, 1), :] for k in range(STEP)]
                for slot, value in zip(slots, values):
                    patch[pl.ds(slot, 1), :] = value
                return carry

            lax.fori_loop(0, (aux_ref[b, o, 0, cap] + STEP - 1) // STEP, rows, 0)

        return carry

    lax.fori_loop(0, 2 * n_py, one, 0)
    for c in range(per_row):
        image[:, c * tile : (c + 1) * tile] = patch[pl.ds(c, PATCH, stride=per_row), :].astype(bf16)

    pixels = image[...].astype(f32)
    row_sign = 1.0 - 2.0 * (lax.broadcasted_iota(jnp.int32, (n, 1), 0) % 2).astype(f32)
    col_sign = 1.0 - 2.0 * (lax.broadcasted_iota(jnp.int32, (1, n), 1) % 2).astype(f32)
    row_edge = jnp.sum(pixels * row_sign, axis=0, keepdims=True) * (1.0 / n)

    def write_real(start, value):
        sign = 1.0 - 2.0 * (lax.broadcasted_iota(jnp.int32, (value.shape[0], 1), 0) % 2).astype(f32)
        fields[0, pl.ds(start, value.shape[0]), :] = (value + sign * row_edge).astype(bf16)

    def write_imag(start, value):
        own = image[pl.ds(start, value.shape[0]), :].astype(f32)
        col_edge = jnp.sum(own * col_sign, axis=1, keepdims=True) * (1.0 / n)
        fields[1, pl.ds(start, value.shape[0]), :] = (-value - col_edge * col_sign).astype(bf16)

    blocked_dot(n, image, slope, write_real)
    blocked_dot(n, slope, image, write_imag)

    def write_halves(start, value):
        halves[pl.ds(start, value.shape[0]), :] = value.astype(bf16)

    def write_spectrum(start, value):
        spectrum[pl.ds(start, value.shape[0]), :] = value

    blocked_dot(n, image, forward, write_halves)
    blocked_dot(2 * n, down, halves, write_spectrum)

    first = lax.broadcasted_iota(jnp.int32, (1, h), 1) == 0
    block = 64

    def multiply(t, carry):
        start = pl.multiple_of(t * block, block)
        low = pl.ds(start, block)
        high = pl.ds(pl.multiple_of(start + n, block), block)
        z_r = spectrum[low, :h] - jnp.where(first, 0.0, spectrum[high, h:])
        z_i = -(spectrum[high, :h] + jnp.where(first, 0.0, spectrum[low, h:]))
        e_r = spectrum[low, h : h + 128]
        e_i = -spectrum[high, h : h + 128]
        for s in range(2):
            k_r, k_i = weights[2 * s, low, :], weights[2 * s + 1, low, :]
            q_r, q_i = edge[2 * s, low, :], edge[2 * s + 1, low, :]
            g_r = k_r * z_r - k_i * z_i
            g_i = k_r * z_i + k_i * z_r
            top_r = q_r * e_r - q_i * e_i
            top_i = q_r * e_i + q_i * e_r
            spectra[low, s * h : s * h + 128] = (g_r[:, :128] - top_i).astype(bf16)
            spectra[low, s * h + 128 : (s + 1) * h] = g_r[:, 128:].astype(bf16)
            spectra[high, s * h : s * h + 128] = (g_i[:, :128] + top_r).astype(bf16)
            spectra[high, s * h + 128 : (s + 1) * h] = g_i[:, 128:].astype(bf16)
        return carry

    lax.fori_loop(0, n // block, multiply, 0)

    for part in range(2):

        def write_columns(start, value, part=part):
            rows = pl.ds(start, value.shape[0])
            for s in range(2):
                columns[s, rows, part * h : (part + 1) * h] = value[:, s * h : (s + 1) * h].astype(bf16)

        blocked_dot(n, back_rows.at[part], spectra, write_columns)
    for s in range(2):

        def write_three(start, value, s=s):
            fields[2 + s, pl.ds(start, value.shape[0]), :] = value.astype(bf16)

        blocked_dot(n, columns.at[s], back_cols, write_three)


def patch_fields(n_px, n_py, tiles, aux):
    vmem = pl.BlockSpec(memory_space=pltpu.VMEM)
    smem = pl.BlockSpec(memory_space=pltpu.SMEM)
    tile = tiles.shape[3]
    n = PATCH
    forward, down, back_rows, back_cols, slope, weights, edge = transform_tables(n)
    return pl.pallas_call(
        functools.partial(fields_kernel, n_px, n_py),
        out_shape=jax.ShapeDtypeStruct((4, n, n), jnp.bfloat16),
        in_specs=[vmem, smem] + [vmem] * 7,
        out_specs=vmem,
        scratch_shapes=[
            pltpu.VMEM((tiles.shape[2], tile), jnp.float32),
            pltpu.VMEM((n * n // tile + 8, tile), jnp.float32),
            pltpu.VMEM((n, n), jnp.bfloat16),
            pltpu.VMEM((n, n), jnp.bfloat16),
            pltpu.VMEM((2 * n, n), jnp.float32),
            pltpu.VMEM((2 * n, n), jnp.bfloat16),
            pltpu.VMEM((2, n, n), jnp.bfloat16),
        ],
        compiler_params=pltpu.CompilerParams(vmem_limit_bytes=40 * 2**20),
        name="patch_fields",
    )(tiles, aux, forward, down, back_rows.reshape(2, n, 2 * n), back_cols, slope, weights, edge)


def halo_kernel(n_px, n_py, fields, out, from_rows, from_cols, corners, send_v, recv_v, send_h, recv_h):
    i = lax.axis_index("px")
    j = lax.axis_index("py")
    width = from_rows.shape[2]
    n = PATCH
    f32, bf16 = jnp.float32, jnp.bfloat16
    has = [i > 0, i < n_px - 1, j > 0, j < n_py - 1]
    beside = [(i - 1, j), (i + 1, j), (i, j - 1), (i, j + 1)]
    barrier = pltpu.get_barrier_semaphore()
    for there, device in zip(has, beside):

        @pl.when(there)
        def _():
            pl.semaphore_signal(barrier, inc=1, device_id=device, device_id_type=MESH)

    pl.semaphore_wait(barrier, sum(there.astype(jnp.int32) for there in has))

    ends = [pl.ds(0, width), pl.ds(n - width, width)]
    inner = pl.ds(width, n - 2 * width)

    def row_copy(side):
        return pltpu.make_async_remote_copy(
            src_ref=fields.at[:, ends[side], :],
            dst_ref=from_rows.at[1 - side],
            send_sem=send_v.at[side],
            recv_sem=recv_v.at[1 - side],
            device_id=beside[side],
            device_id_type=MESH,
        )

    def col_copy(side, piece):
        rows = [ends[0], ends[1], inner][piece]
        source = fields.at[:, inner, ends[side]] if piece == 2 else corners.at[side, :, rows, :]
        return pltpu.make_async_remote_copy(
            src_ref=source,
            dst_ref=from_cols.at[1 - side, :, rows, :],
            send_sem=send_h.at[side, piece],
            recv_sem=recv_h.at[1 - side, piece],
            device_id=beside[2 + side],
            device_id_type=MESH,
        )

    for side in range(2):

        @pl.when(has[side])
        def _():
            row_copy(side).start()

    for side in range(2):

        @pl.when(has[2 + side])
        def _():
            col_copy(side, 2).start()

    out[:, inner, :] = fields[:, inner, :].astype(f32)
    rise = (lax.broadcasted_iota(jnp.int32, (1, width, 1), 1).astype(f32) + 0.5) * (1.0 / width)
    fall = (width - 0.5 - lax.broadcasted_iota(jnp.int32, (1, width, 1), 1).astype(f32)) * (1.0 / width)
    for side, ramp in enumerate((rise, fall)):
        rows = ends[side]

        @pl.when(has[side])
        def _():
            pltpu.make_async_remote_copy(
                src_ref=fields.at[:, ends[1 - side], :],
                dst_ref=from_rows.at[side],
                send_sem=send_v.at[1 - side],
                recv_sem=recv_v.at[side],
                device_id=beside[side],
                device_id_type=MESH,
            ).wait_recv()
            out[:, rows, :] = ramp * fields[:, rows, :].astype(f32) + (1.0 - ramp) * from_rows[side].astype(f32)

        @pl.when(jnp.logical_not(has[side]))
        def _():
            out[:, rows, :] = fields[:, rows, :].astype(f32)

        for other in range(2):
            corners[other, :, rows, :] = out[:, rows, ends[other]].astype(bf16)

            @pl.when(has[2 + other])
            def _():
                col_copy(other, side).start()

    rise = (lax.broadcasted_iota(jnp.int32, (1, 1, width), 2).astype(f32) + 0.5) * (1.0 / width)
    fall = (width - 0.5 - lax.broadcasted_iota(jnp.int32, (1, 1, width), 2).astype(f32)) * (1.0 / width)
    for piece in (2, 0, 1):
        rows = [ends[0], ends[1], inner][piece]
        for side, ramp in enumerate((rise, fall)):

            @pl.when(has[2 + side])
            def _():
                pltpu.make_async_remote_copy(
                    src_ref=corners.at[1 - side, :, rows, :],
                    dst_ref=from_cols.at[side, :, rows, :],
                    send_sem=send_h.at[1 - side, piece],
                    recv_sem=recv_h.at[side, piece],
                    device_id=beside[2 + side],
                    device_id_type=MESH,
                ).wait_recv()
                out[:, rows, ends[side]] = ramp * out[:, rows, ends[side]] + (1.0 - ramp) * from_cols[
                    side, :, rows, :
                ].astype(f32)

    for side in range(2):

        @pl.when(has[side])
        def _():
            row_copy(side).wait_send()

        @pl.when(has[2 + side])
        def _():
            for piece in range(3):
                col_copy(side, piece).wait_send()


def blend(n_px, n_py, fields, width):
    vmem = pl.BlockSpec(memory_space=pltpu.VMEM)
    n = PATCH
    return pl.pallas_call(
        functools.partial(halo_kernel, n_px, n_py),
        out_shape=jax.ShapeDtypeStruct((4, n, n), jnp.float32),
        in_specs=[vmem],
        out_specs=vmem,
        scratch_shapes=[
            pltpu.VMEM((2, 4, width, n), jnp.bfloat16),
            pltpu.VMEM((2, 4, n, width), jnp.bfloat16),
            pltpu.VMEM((2, 4, n, width), jnp.bfloat16),
            pltpu.SemaphoreType.DMA((2,)),
            pltpu.SemaphoreType.DMA((2,)),
            pltpu.SemaphoreType.DMA((2, 3)),
            pltpu.SemaphoreType.DMA((2, 3)),
        ],
        compiler_params=pltpu.CompilerParams(
            collective_id=1, has_side_effects=True, vmem_limit_bytes=40 * 2**20
        ),
        name="halo_blend",
    )(fields)


def on_device(kappa, send_list, dest_slot, send_count):
    n_px = lax.axis_size("px")
    n_py = lax.axis_size("py")
    tiles, aux = gather_tiles(n_px, n_py, kappa, send_list, dest_slot, send_count)
    tiles, aux = exchange(n_px, n_py, tiles, aux)
    fields = patch_fields(n_px, n_py, tiles, aux)
    return blend(n_px, n_py, fields, kappa.shape[1])


def solution(mesh):
    placed = (
        P(("px", "py"), None),
        P(("px", "py"), None, None),
        P(("px", "py"), None, None),
        P(("px", "py"), None),
    )
    return jax.shard_map(
        on_device, mesh=mesh, in_specs=placed, out_specs=P(None, "px", "py"), check_vma=False
    )
```

```python
import functools
import math

import jax
import jax.numpy as jnp
import numpy as np
from jax import lax
from jax.experimental import pallas as pl
from jax.experimental.pallas import tpu as pltpu
from jax.sharding import PartitionSpec as P

PATCH = 512
MESH = pl.DeviceIdType.MESH
STEP = 16
TABLES = 7


def exchange_kernel(
    n_px, n_py, kappa, lists, slots, counts, got_tiles, got_aux,
    held, wide, stage, tiles, aux, rows, marks, totals, load, send_t, recv_t, send_a, recv_a, local,
):
    i = lax.axis_index("px")
    j = lax.axis_index("py")
    cap = rows.shape[2]
    has_up = i > 0
    has_down = i < n_px - 1
    upper = jnp.maximum(i - 1, 0)
    loads = [
        pltpu.make_async_copy(kappa, held, load.at[0]),
        pltpu.make_async_copy(counts, totals, load.at[1]),
    ]
    for b, band in enumerate((i, upper)):
        part = pl.ds(pl.multiple_of(band * n_py, n_py), n_py)
        loads.append(pltpu.make_async_copy(lists.at[0, part], rows.at[b], load.at[2 + b]))
        loads.append(pltpu.make_async_copy(slots.at[0, part], marks.at[b], load.at[4 + b]))
    for copy in loads:
        copy.start()
    barrier = pltpu.get_barrier_semaphore()
    for o in range(1, n_py):
        pl.semaphore_signal(barrier, inc=1, device_id=(i, lax.rem(j + o, n_py)), device_id_type=MESH)

    @pl.when(has_down)
    def _():
        for o in range(n_py):
            pl.semaphore_signal(
                barrier, inc=1, device_id=(i + 1, lax.rem(j + o, n_py)), device_id_type=MESH
            )

    for copy in loads:
        copy.wait()
    wide[...] = held[...].astype(jnp.float32)
    pl.semaphore_wait(barrier, n_py - 1 + jnp.where(has_up, n_py, 0))

    def copies(b, o):
        target = (i - b, lax.rem(j + o, n_py))
        return [
            pltpu.make_async_remote_copy(
                src_ref=source.at[b, o],
                dst_ref=landing.at[b, o],
                send_sem=send.at[b, o],
                recv_sem=recv.at[b, o],
                device_id=target,
                device_id_type=MESH,
            )
            for source, landing, send, recv in (
                (tiles, got_tiles, send_t, recv_t),
                (aux, got_aux, send_a, recv_a),
            )
        ]

    own = [
        pltpu.make_async_copy(tiles.at[0, 0], got_tiles.at[0, 0], local.at[0]),
        pltpu.make_async_copy(aux.at[0, 0], got_aux.at[0, 0], local.at[1]),
    ]
    lanes = lax.broadcasted_iota(jnp.int32, (1, cap), 1)
    dump = PATCH * PATCH // wide.shape[1]

    def collect(b, o):
        column = lax.rem(j + o, n_py)

        def some(c, carry):
            base = pl.multiple_of(c * STEP, STEP)
            sources = [rows[b, column, base + k] for k in range(STEP)]
            values = [wide[pl.ds(source, 1), :] for source in sources]
            for k in range(STEP):
                stage[pl.ds(base + k, 1), :] = values[k]
            return carry

        lax.fori_loop(0, cap // STEP, some, 0)
        tiles[b, o] = stage[...].astype(jnp.bfloat16)
        count = totals[0, (i if b == 0 else upper) * n_py + column]
        aux[b, o] = jnp.full(aux.shape[2:], count, jnp.int32)
        aux[b, o, :, :cap] = jnp.where(lanes < count, marks[b, pl.ds(column, 1), :], dump)

    def place_of(t):
        step = (t + 1) // 2
        return lax.rem(n_py // 2 + step * (2 * lax.rem(t, 2) - 1) + n_py, n_py)

    def forward(t, carry):
        o = place_of(t)
        collect(0, o)

        @pl.when(o > 0)
        def _():
            for copy in copies(0, o):
                copy.start()

        @pl.when(o == 0)
        def _():
            for copy in own:
                copy.start()

        @pl.when(has_up)
        def _():
            collect(1, o)
            for copy in copies(1, o):
                copy.start()

        return carry

    lax.fori_loop(0, n_py, forward, 0)

    def finish(t, carry):
        o = place_of(t)

        @pl.when(o > 0)
        def _():
            for copy in copies(0, o):
                copy.wait()

        @pl.when(has_up)
        def _():
            for copy in copies(1, o):
                copy.wait_send()

        @pl.when(has_down)
        def _():
            for copy in copies(1, o):
                copy.wait_recv()

        return carry

    lax.fori_loop(0, n_py, finish, 0)
    for copy in own:
        copy.wait()


def exchange(n_px, n_py, kappa, send_list, dest_slot, send_count):
    cap = send_list.shape[2]
    width = (cap + 128) // 128 * 128
    tile = kappa.shape[1]
    hbm = pl.BlockSpec(memory_space=pltpu.HBM)
    vmem = pl.BlockSpec(memory_space=pltpu.VMEM)
    tiles = (2, n_py, cap, tile)
    aux = (2, n_py, 1, width)
    return pl.pallas_call(
        functools.partial(exchange_kernel, n_px, n_py),
        out_shape=(
            jax.ShapeDtypeStruct(tiles, jnp.bfloat16),
            jax.ShapeDtypeStruct(aux, jnp.int32),
        ),
        in_specs=[hbm] * 4,
        out_specs=(vmem, vmem),
        scratch_shapes=[
            pltpu.VMEM(kappa.shape, jnp.bfloat16),
            pltpu.VMEM(kappa.shape, jnp.float32),
            pltpu.VMEM((cap, tile), jnp.float32),
            pltpu.VMEM(tiles, jnp.bfloat16),
            pltpu.VMEM(aux, jnp.int32),
            pltpu.SMEM((2, n_py, cap), jnp.int32),
            pltpu.VMEM((2, n_py, cap), jnp.int32),
            pltpu.SMEM(send_count.shape, jnp.int32),
            pltpu.SemaphoreType.DMA((6,)),
        ]
        + [pltpu.SemaphoreType.DMA((2, n_py))] * 4
        + [pltpu.SemaphoreType.DMA((2,))],
        compiler_params=pltpu.CompilerParams(
            collective_id=0, has_side_effects=True, vmem_limit_bytes=32 * 2**20
        ),
        name="exchange_tiles",
    )(kappa, send_list, dest_slot, send_count)


def dft_tables(length):
    positions = np.arange(length)
    angles = (positions[:, None] * positions[None, :] % length).astype(np.float32) * np.float32(
        2.0 * math.pi / length
    )
    return np.cos(angles).astype(np.float32), np.sin(angles).astype(np.float32)


def wavenumbers(length):
    positions = np.arange(length)
    return (positions - length * (positions >= (length + 1) // 2)).astype(np.float32) * np.float32(2.0 / length)


def transform_tables(n):
    h = n // 2
    cos, sin = dft_tables(n)
    forward = np.concatenate([cos[:, :h], sin[:, :h]], 1)
    forward[:, h] = cos[:, h]
    down = np.concatenate([cos, sin], 0)
    back_rows = np.block([[cos, -sin], [sin, cos]])
    back_cols = np.concatenate([2.0 * cos[:h], -2.0 * sin[:h]], 0)
    back_cols[0] = 1.0
    back_cols[h] = cos[h]
    signed = wavenumbers(n).astype(np.float64)
    order = np.arange(1, h)
    lag = np.arange(n)
    wave = -(2.0 / n) * (signed[1:h] * np.sin(2.0 * np.pi * (lag[:, None] * order % n) / n)).sum(1)
    slope = wave[(lag[None, :] - lag[:, None]) % n]
    across, along = signed[None, :], signed[:, None]
    power = across**2 + along**2
    lens = 1j * (across + 1j * along) ** 3 / np.where(power > 0, power, 1.0) / (n * n)
    mirror = np.conj(lens[-lag % n][:, -lag % n])
    even, odd = (lens + mirror) / 2, (lens - mirror) / 2j
    weights = np.stack([even.real, even.imag, odd.real, odd.imag])
    edge = np.zeros((4, n, 128))
    edge[:, :, 0] = weights[:, :, h]
    bf16 = [jnp.asarray(t, jnp.bfloat16) for t in (forward, down, back_rows, back_cols, slope)]
    return *bf16, jnp.asarray(weights[:, :, :h], jnp.float32), jnp.asarray(edge, jnp.float32)


def blocked_dot(rows, left, right, write, block=256):
    def one(t, carry):
        start = pl.multiple_of(t * block, block)
        write(start, jnp.dot(left[pl.ds(start, block), :], right[...], preferred_element_type=jnp.float32))
        return carry

    lax.fori_loop(0, rows // block, one, 0)


def fields_kernel(
    n_px, n_py, tiles_ref, aux_hbm, *rest
):
    sources, fields = rest[:TABLES], rest[TABLES]
    held = rest[TABLES + 1 : 2 * TABLES + 1]
    slope, forward, down, weights, edge, back_rows, back_cols = held
    wide, patch, image, halves, spectrum, spectra, columns, aux_ref, load = rest[2 * TABLES + 1 :]
    loads = [pltpu.make_async_copy(aux_hbm, aux_ref, load.at[TABLES])]
    loads += [pltpu.make_async_copy(a, b, load.at[k]) for k, (a, b) in enumerate(zip(sources, held))]
    for copy in loads:
        copy.start()
    loads[0].wait()
    i = lax.axis_index("px")
    cap = tiles_ref.shape[2]
    tile = tiles_ref.shape[3]
    per_row = PATCH // tile
    n, h = PATCH, PATCH // 2
    bf16, f32 = jnp.bfloat16, jnp.float32

    def one(t, carry):
        b = t // n_py
        o = lax.rem(t, n_py)
        live = jnp.logical_or(b == 0, i < n_px - 1)

        @pl.when(live)
        def _():
            wide[...] = tiles_ref[b, o].astype(f32)

            def rows(c, carry):
                base = pl.multiple_of(c * STEP, STEP)
                slots = [aux_ref[b, o, 0, base + k] for k in range(STEP)]
                values = [wide[pl.ds(base + k, 1), :] for k in range(STEP)]
                for slot, value in zip(slots, values):
                    patch[pl.ds(slot, 1), :] = value
                return carry

            lax.fori_loop(0, (aux_ref[b, o, 0, cap] + STEP - 1) // STEP, rows, 0)

        return carry

    lax.fori_loop(0, 2 * n_py, one, 0)
    for c in range(per_row):
        image[:, c * tile : (c + 1) * tile] = patch[pl.ds(c, PATCH, stride=per_row), :].astype(bf16)

    for copy in loads[1:]:
        copy.wait()

    pixels = image[...].astype(f32)
    row_sign = 1.0 - 2.0 * (lax.broadcasted_iota(jnp.int32, (n, 1), 0) % 2).astype(f32)
    col_sign = 1.0 - 2.0 * (lax.broadcasted_iota(jnp.int32, (1, n), 1) % 2).astype(f32)
    row_edge = jnp.sum(pixels * row_sign, axis=0, keepdims=True) * (1.0 / n)

    def write_real(start, value):
        sign = 1.0 - 2.0 * (lax.broadcasted_iota(jnp.int32, (value.shape[0], 1), 0) % 2).astype(f32)
        fields[0, pl.ds(start, value.shape[0]), :] = (value + sign * row_edge).astype(bf16)

    def write_imag(start, value):
        own = image[pl.ds(start, value.shape[0]), :].astype(f32)
        col_edge = jnp.sum(own * col_sign, axis=1, keepdims=True) * (1.0 / n)
        fields[1, pl.ds(start, value.shape[0]), :] = (-value - col_edge * col_sign).astype(bf16)

    blocked_dot(n, image, slope, write_real)
    blocked_dot(n, slope, image, write_imag)

    def write_halves(start, value):
        halves[pl.ds(start, value.shape[0]), :] = value.astype(bf16)

    def write_spectrum(start, value):
        spectrum[pl.ds(start, value.shape[0]), :] = value

    blocked_dot(n, image, forward, write_halves)
    blocked_dot(2 * n, down, halves, write_spectrum)

    first = lax.broadcasted_iota(jnp.int32, (1, h), 1) == 0
    block = 64

    def multiply(t, carry):
        start = pl.multiple_of(t * block, block)
        low = pl.ds(start, block)
        high = pl.ds(pl.multiple_of(start + n, block), block)
        z_r = spectrum[low, :h] - jnp.where(first, 0.0, spectrum[high, h:])
        z_i = -(spectrum[high, :h] + jnp.where(first, 0.0, spectrum[low, h:]))
        e_r = spectrum[low, h : h + 128]
        e_i = -spectrum[high, h : h + 128]
        for s in range(2):
            k_r, k_i = weights[2 * s, low, :], weights[2 * s + 1, low, :]
            q_r, q_i = edge[2 * s, low, :], edge[2 * s + 1, low, :]
            g_r = k_r * z_r - k_i * z_i
            g_i = k_r * z_i + k_i * z_r
            top_r = q_r * e_r - q_i * e_i
            top_i = q_r * e_i + q_i * e_r
            spectra[low, s * h : s * h + 128] = (g_r[:, :128] - top_i).astype(bf16)
            spectra[low, s * h + 128 : (s + 1) * h] = g_r[:, 128:].astype(bf16)
            spectra[high, s * h : s * h + 128] = (g_i[:, :128] + top_r).astype(bf16)
            spectra[high, s * h + 128 : (s + 1) * h] = g_i[:, 128:].astype(bf16)
        return carry

    lax.fori_loop(0, n // block, multiply, 0)

    for part in range(2):

        def write_columns(start, value, part=part):
            rows = pl.ds(start, value.shape[0])
            for s in range(2):
                columns[s, rows, part * h : (part + 1) * h] = value[:, s * h : (s + 1) * h].astype(bf16)

        blocked_dot(n, back_rows.at[part], spectra, write_columns)
    for s in range(2):

        def write_three(start, value, s=s):
            fields[2 + s, pl.ds(start, value.shape[0]), :] = value.astype(bf16)

        blocked_dot(n, columns.at[s], back_cols, write_three)


def patch_fields(n_px, n_py, tiles, aux):
    vmem = pl.BlockSpec(memory_space=pltpu.VMEM)
    tile = tiles.shape[3]
    n = PATCH
    forward, down, back_rows, back_cols, slope, weights, edge = transform_tables(n)
    tables = [slope, forward, down, weights, edge, back_rows.reshape(2, n, 2 * n), back_cols]
    hbm = pl.BlockSpec(memory_space=pltpu.HBM)
    return pl.pallas_call(
        functools.partial(fields_kernel, n_px, n_py),
        out_shape=jax.ShapeDtypeStruct((4, n, n), jnp.bfloat16),
        in_specs=[vmem, hbm] + [hbm] * TABLES,
        out_specs=vmem,
        scratch_shapes=[pltpu.VMEM(table.shape, table.dtype) for table in tables]
        + [
            pltpu.VMEM((tiles.shape[2], tile), jnp.float32),
            pltpu.VMEM((n * n // tile + 8, tile), jnp.float32),
            pltpu.VMEM((n, n), jnp.bfloat16),
            pltpu.VMEM((n, n), jnp.bfloat16),
            pltpu.VMEM((2 * n, n), jnp.float32),
            pltpu.VMEM((2 * n, n), jnp.bfloat16),
            pltpu.VMEM((2, n, n), jnp.bfloat16),
            pltpu.SMEM(aux.shape, aux.dtype),
            pltpu.SemaphoreType.DMA((TABLES + 1,)),
        ],
        compiler_params=pltpu.CompilerParams(vmem_limit_bytes=40 * 2**20),
        name="patch_fields",
    )(tiles, aux, *tables)


def halo_kernel(n_px, n_py, fields, out, from_rows, from_cols, corners, send_v, recv_v, send_h, recv_h):
    i = lax.axis_index("px")
    j = lax.axis_index("py")
    width = from_rows.shape[2]
    n = PATCH
    f32, bf16 = jnp.float32, jnp.bfloat16
    has = [i > 0, i < n_px - 1, j > 0, j < n_py - 1]
    beside = [(i - 1, j), (i + 1, j), (i, j - 1), (i, j + 1)]
    barrier = pltpu.get_barrier_semaphore()
    for there, device in zip(has, beside):

        @pl.when(there)
        def _():
            pl.semaphore_signal(barrier, inc=1, device_id=device, device_id_type=MESH)

    pl.semaphore_wait(barrier, sum(there.astype(jnp.int32) for there in has))

    ends = [pl.ds(0, width), pl.ds(n - width, width)]
    inner = pl.ds(width, n - 2 * width)

    def row_copy(side):
        return pltpu.make_async_remote_copy(
            src_ref=fields.at[:, ends[side], :],
            dst_ref=from_rows.at[1 - side],
            send_sem=send_v.at[side],
            recv_sem=recv_v.at[1 - side],
            device_id=beside[side],
            device_id_type=MESH,
        )

    def col_copy(side, piece):
        rows = [ends[0], ends[1], inner][piece]
        source = fields.at[:, inner, ends[side]] if piece == 2 else corners.at[side, :, rows, :]
        return pltpu.make_async_remote_copy(
            src_ref=source,
            dst_ref=from_cols.at[1 - side, :, rows, :],
            send_sem=send_h.at[side, piece],
            recv_sem=recv_h.at[1 - side, piece],
            device_id=beside[2 + side],
            device_id_type=MESH,
        )

    for side in range(2):

        @pl.when(has[side])
        def _():
            row_copy(side).start()

    for side in range(2):

        @pl.when(has[2 + side])
        def _():
            col_copy(side, 2).start()

    out[:, inner, :] = fields[:, inner, :].astype(f32)
    rise = (lax.broadcasted_iota(jnp.int32, (1, width, 1), 1).astype(f32) + 0.5) * (1.0 / width)
    fall = (width - 0.5 - lax.broadcasted_iota(jnp.int32, (1, width, 1), 1).astype(f32)) * (1.0 / width)
    for side, ramp in enumerate((rise, fall)):
        rows = ends[side]

        @pl.when(has[side])
        def _():
            pltpu.make_async_remote_copy(
                src_ref=fields.at[:, ends[1 - side], :],
                dst_ref=from_rows.at[side],
                send_sem=send_v.at[1 - side],
                recv_sem=recv_v.at[side],
                device_id=beside[side],
                device_id_type=MESH,
            ).wait_recv()
            out[:, rows, :] = ramp * fields[:, rows, :].astype(f32) + (1.0 - ramp) * from_rows[side].astype(f32)

        @pl.when(jnp.logical_not(has[side]))
        def _():
            out[:, rows, :] = fields[:, rows, :].astype(f32)

        for other in range(2):
            corners[other, :, rows, :] = out[:, rows, ends[other]].astype(bf16)

            @pl.when(has[2 + other])
            def _():
                col_copy(other, side).start()

    rise = (lax.broadcasted_iota(jnp.int32, (1, 1, width), 2).astype(f32) + 0.5) * (1.0 / width)
    fall = (width - 0.5 - lax.broadcasted_iota(jnp.int32, (1, 1, width), 2).astype(f32)) * (1.0 / width)
    for piece in (2, 0, 1):
        rows = [ends[0], ends[1], inner][piece]
        for side, ramp in enumerate((rise, fall)):

            @pl.when(has[2 + side])
            def _():
                pltpu.make_async_remote_copy(
                    src_ref=corners.at[1 - side, :, rows, :],
                    dst_ref=from_cols.at[side, :, rows, :],
                    send_sem=send_h.at[1 - side, piece],
                    recv_sem=recv_h.at[side, piece],
                    device_id=beside[2 + side],
                    device_id_type=MESH,
                ).wait_recv()
                out[:, rows, ends[side]] = ramp * out[:, rows, ends[side]] + (1.0 - ramp) * from_cols[
                    side, :, rows, :
                ].astype(f32)

    for side in range(2):

        @pl.when(has[side])
        def _():
            row_copy(side).wait_send()

        @pl.when(has[2 + side])
        def _():
            for piece in range(3):
                col_copy(side, piece).wait_send()


def blend(n_px, n_py, fields, width):
    vmem = pl.BlockSpec(memory_space=pltpu.VMEM)
    n = PATCH
    return pl.pallas_call(
        functools.partial(halo_kernel, n_px, n_py),
        out_shape=jax.ShapeDtypeStruct((4, n, n), jnp.float32),
        in_specs=[vmem],
        out_specs=vmem,
        scratch_shapes=[
            pltpu.VMEM((2, 4, width, n), jnp.bfloat16),
            pltpu.VMEM((2, 4, n, width), jnp.bfloat16),
            pltpu.VMEM((2, 4, n, width), jnp.bfloat16),
            pltpu.SemaphoreType.DMA((2,)),
            pltpu.SemaphoreType.DMA((2,)),
            pltpu.SemaphoreType.DMA((2, 3)),
            pltpu.SemaphoreType.DMA((2, 3)),
        ],
        compiler_params=pltpu.CompilerParams(
            collective_id=1, has_side_effects=True, vmem_limit_bytes=40 * 2**20
        ),
        name="halo_blend",
    )(fields)


def on_device(kappa, send_list, dest_slot, send_count):
    n_px = lax.axis_size("px")
    n_py = lax.axis_size("py")
    tiles, aux = exchange(n_px, n_py, kappa, send_list, dest_slot, send_count)
    fields = patch_fields(n_px, n_py, tiles, aux)
    return blend(n_px, n_py, fields, kappa.shape[1])


def solution(mesh):
    placed = (
        P(("px", "py"), None),
        P(("px", "py"), None, None),
        P(("px", "py"), None, None),
        P(("px", "py"), None),
    )
    return jax.shard_map(
        on_device, mesh=mesh, in_specs=placed, out_specs=P(None, "px", "py"), check_vma=False
    )
```

```python
import functools
import math

import jax
import jax.numpy as jnp
import numpy as np
from jax import lax
from jax.experimental import pallas as pl
from jax.experimental.pallas import tpu as pltpu
from jax.sharding import PartitionSpec as P

PATCH = 512
MESH = pl.DeviceIdType.MESH
STEP = 16
PLACE = 512
TABLES = 7


def dft_tables(length):
    positions = np.arange(length)
    angles = (positions[:, None] * positions[None, :] % length).astype(np.float32) * np.float32(
        2.0 * math.pi / length
    )
    return np.cos(angles).astype(np.float32), np.sin(angles).astype(np.float32)


def wavenumbers(length):
    positions = np.arange(length)
    return (positions - length * (positions >= (length + 1) // 2)).astype(np.float32) * np.float32(2.0 / length)


def transform_tables(n):
    h = n // 2
    cos, sin = dft_tables(n)
    forward = np.concatenate([cos[:, :h], sin[:, :h]], 1)
    forward[:, h] = cos[:, h]
    down = np.concatenate([cos, sin], 0)
    back_rows = np.block([[cos, -sin], [sin, cos]])
    back_cols = np.concatenate([2.0 * cos[:h], -2.0 * sin[:h]], 0)
    back_cols[0] = 1.0
    back_cols[h] = cos[h]
    signed = wavenumbers(n).astype(np.float64)
    order = np.arange(1, h)
    lag = np.arange(n)
    wave = -(2.0 / n) * (signed[1:h] * np.sin(2.0 * np.pi * (lag[:, None] * order % n) / n)).sum(1)
    slope = wave[(lag[None, :] - lag[:, None]) % n]
    across, along = signed[None, :], signed[:, None]
    power = across**2 + along**2
    lens = 1j * (across + 1j * along) ** 3 / np.where(power > 0, power, 1.0) / (n * n)
    mirror = np.conj(lens[-lag % n][:, -lag % n])
    even, odd = (lens + mirror) / 2, (lens - mirror) / 2j
    weights = np.stack([even.real, even.imag, odd.real, odd.imag])
    edge = np.zeros((4, n, 128))
    edge[:, :, 0] = weights[:, :, h]
    bf16 = [jnp.asarray(t, jnp.bfloat16) for t in (forward, down, back_rows, back_cols, slope)]
    return *bf16, jnp.asarray(weights[:, :, :h], jnp.float32), jnp.asarray(edge, jnp.float32)


def blocked_dot(rows, left, right, write, block=256):
    def one(t, carry):
        start = pl.multiple_of(t * block, block)
        write(start, jnp.dot(left[pl.ds(start, block), :], right[...], preferred_element_type=jnp.float32))
        return carry

    lax.fori_loop(0, rows // block, one, 0)


def flexion_kernel(n_px, n_py, kappa, lists, slots, counts, *rest):
    sources, (out,), rest = rest[:TABLES], rest[TABLES : TABLES + 1], rest[TABLES + 1 :]
    slope, forward, down, weights, edge, back_rows, back_cols = tables = rest[:TABLES]
    (
        held, wide, stage, tiles, aux, got_tiles, got_aux, rows, marks, totals,
        patch, image, halves, spectrum, spectra, columns, fields, from_rows, from_cols, corners,
        load, send_t, recv_t, send_a, recv_a, send_v, recv_v, send_h, recv_h,
    ) = rest[TABLES:]
    i = lax.axis_index("px")
    j = lax.axis_index("py")
    cap = rows.shape[2]
    tile = wide.shape[1]
    n, h = PATCH, PATCH // 2
    slot_count = n * n // tile
    f32, bf16 = jnp.float32, jnp.bfloat16
    has_up, has_down = i > 0, i < n_px - 1
    upper = jnp.maximum(i - 1, 0)

    loads = [
        pltpu.make_async_copy(kappa, held, load.at[0]),
        pltpu.make_async_copy(counts, totals, load.at[1]),
    ]
    for b, band in enumerate((i, upper)):
        part = pl.ds(pl.multiple_of(band * n_py, n_py), n_py)
        loads.append(pltpu.make_async_copy(lists.at[0, part], rows.at[b], load.at[2 + b]))
        loads.append(pltpu.make_async_copy(slots.at[0, part], marks.at[b], load.at[4 + b]))
    table_loads = [
        pltpu.make_async_copy(a, b, load.at[6 + k]) for k, (a, b) in enumerate(zip(sources, tables))
    ]
    for copy in loads:
        copy.start()

    barrier = pltpu.get_barrier_semaphore()
    for o in range(1, n_py):
        pl.semaphore_signal(barrier, inc=1, device_id=(i, lax.rem(j + o, n_py)), device_id_type=MESH)

    @pl.when(has_down)
    def _():
        for o in range(n_py):
            pl.semaphore_signal(
                barrier, inc=1, device_id=(i + 1, lax.rem(j + o, n_py)), device_id_type=MESH
            )

    @pl.when(has_up)
    def _():
        pl.semaphore_signal(barrier, inc=1, device_id=(i - 1, j), device_id_type=MESH)

    for copy in loads:
        copy.wait()
    for copy in table_loads:
        copy.start()
    wide[...] = held[...].astype(f32)
    patch[...] = jnp.zeros_like(patch)
    pl.semaphore_wait(
        barrier, n_py - 1 + jnp.where(has_up, n_py, 0) + jnp.where(has_down, 1, 0)
    )

    def copies(b, o):
        target = (i - b, lax.rem(j + o, n_py))
        return [
            pltpu.make_async_remote_copy(
                src_ref=source.at[b, o],
                dst_ref=landing.at[b, o],
                send_sem=send.at[b, o],
                recv_sem=recv.at[b, o],
                device_id=target,
                device_id_type=MESH,
            )
            for source, landing, send, recv in (
                (tiles, got_tiles, send_t, recv_t),
                (aux, got_aux, send_a, recv_a),
            )
        ]

    lanes = lax.broadcasted_iota(jnp.int32, (1, cap), 1)

    def collect(b, o):
        column = lax.rem(j + o, n_py)

        def some(c, carry):
            base = pl.multiple_of(c * STEP, STEP)
            picks = [rows[b, column, base + k] for k in range(STEP)]
            values = [wide[pl.ds(pick, 1), :] for pick in picks]
            for k in range(STEP):
                stage[pl.ds(base + k, 1), :] = values[k]
            return carry

        lax.fori_loop(0, cap // STEP, some, 0)
        tiles[b, o] = stage[...].astype(bf16)
        count = totals[0, (i if b == 0 else upper) * n_py + column]
        aux[b, o] = jnp.where(lanes < count, marks[b, pl.ds(column, 1), :], slot_count)

    def place_of(t):
        step = (t + 1) // 2
        return lax.rem(n_py // 2 + step * (2 * lax.rem(t, 2) - 1) + n_py, n_py)

    def deliver(t, carry):
        o = place_of(t)
        collect(0, o)

        @pl.when(o > 0)
        def _():
            for copy in copies(0, o):
                copy.start()

        @pl.when(has_up)
        def _():
            collect(1, o)
            for copy in copies(1, o):
                copy.start()

        return carry

    lax.fori_loop(0, n_py, deliver, 0)

    def place(values, targets):
        def part(r, carry):
            base = pl.multiple_of(r * PLACE, PLACE)
            ids = lax.broadcasted_iota(jnp.int32, (PLACE, cap), 0) + base
            chosen = jnp.where(ids == targets, 1.0, 0.0).astype(bf16)
            patch[pl.ds(base, PLACE), :] += jnp.dot(chosen, values, preferred_element_type=f32)
            return carry

        lax.fori_loop(0, slot_count // PLACE, part, 0)

    def receive(t, carry):
        o = place_of(t)

        @pl.when(o == 0)
        def _():
            place(tiles[0, 0], aux[0, 0])

        @pl.when(o > 0)
        def _():
            for copy in copies(0, o):
                copy.wait_recv()
            place(got_tiles[0, o], got_aux[0, o])

        @pl.when(has_down)
        def _():
            for copy in copies(1, o):
                copy.wait_recv()
            place(got_tiles[1, o], got_aux[1, o])

        return carry

    lax.fori_loop(0, n_py, receive, 0)
    per_row = n // tile
    for c in range(per_row):
        image[:, c * tile : (c + 1) * tile] = patch[pl.ds(c, n, stride=per_row), :].astype(bf16)
    for copy in table_loads:
        copy.wait()

    width = tile
    has = [has_up, has_down, j > 0, j < n_py - 1]
    beside = [(i - 1, j), (i + 1, j), (i, j - 1), (i, j + 1)]
    ends = [pl.ds(0, width), pl.ds(n - width, width)]
    inner = pl.ds(width, n - 2 * width)
    pairs = [pl.ds(0, 2), pl.ds(2, 2)]

    def row_copy(side, pair):
        return pltpu.make_async_remote_copy(
            src_ref=fields.at[pairs[pair], ends[side], :],
            dst_ref=from_rows.at[1 - side, pairs[pair]],
            send_sem=send_v.at[side, pair],
            recv_sem=recv_v.at[1 - side, pair],
            device_id=beside[side],
            device_id_type=MESH,
        )

    def col_copy(side, piece):
        if piece < 2:
            part, span = pl.ds(0, 4), ends[piece]
            source = corners.at[side, :, span, :]
        else:
            part, span = pairs[piece - 2], inner
            source = fields.at[part, inner, ends[side]]
        return pltpu.make_async_remote_copy(
            src_ref=source,
            dst_ref=from_cols.at[1 - side, part, span, :],
            send_sem=send_h.at[side, piece],
            recv_sem=recv_h.at[1 - side, piece],
            device_id=beside[2 + side],
            device_id_type=MESH,
        )

    def send_strips(pair):
        for side in range(2):

            @pl.when(has[side])
            def _():
                row_copy(side, pair).start()

            @pl.when(has[2 + side])
            def _():
                col_copy(side, 2 + pair).start()

    pixels = image[...].astype(f32)
    row_sign = 1.0 - 2.0 * (lax.broadcasted_iota(jnp.int32, (n, 1), 0) % 2).astype(f32)
    col_sign = 1.0 - 2.0 * (lax.broadcasted_iota(jnp.int32, (1, n), 1) % 2).astype(f32)
    row_edge = jnp.sum(pixels * row_sign, axis=0, keepdims=True) * (1.0 / n)

    def write_real(start, value):
        sign = 1.0 - 2.0 * (lax.broadcasted_iota(jnp.int32, (value.shape[0], 1), 0) % 2).astype(f32)
        fields[0, pl.ds(start, value.shape[0]), :] = (value + sign * row_edge).astype(bf16)

    def write_imag(start, value):
        own = image[pl.ds(start, value.shape[0]), :].astype(f32)
        col_edge = jnp.sum(own * col_sign, axis=1, keepdims=True) * (1.0 / n)
        fields[1, pl.ds(start, value.shape[0]), :] = (-value - col_edge * col_sign).astype(bf16)

    blocked_dot(n, image, slope, write_real)
    blocked_dot(n, slope, image, write_imag)
    send_strips(0)

    def write_halves(start, value):
        halves[pl.ds(start, value.shape[0]), :] = value.astype(bf16)

    def write_spectrum(start, value):
        spectrum[pl.ds(start, value.shape[0]), :] = value

    blocked_dot(n, image, forward, write_halves)
    blocked_dot(2 * n, down, halves, write_spectrum)

    first = lax.broadcasted_iota(jnp.int32, (1, h), 1) == 0
    block = 64

    def multiply(t, carry):
        start = pl.multiple_of(t * block, block)
        low = pl.ds(start, block)
        high = pl.ds(pl.multiple_of(start + n, block), block)
        z_r = spectrum[low, :h] - jnp.where(first, 0.0, spectrum[high, h:])
        z_i = -(spectrum[high, :h] + jnp.where(first, 0.0, spectrum[low, h:]))
        e_r = spectrum[low, h : h + 128]
        e_i = -spectrum[high, h : h + 128]
        for s in range(2):
            k_r, k_i = weights[2 * s, low, :], weights[2 * s + 1, low, :]
            q_r, q_i = edge[2 * s, low, :], edge[2 * s + 1, low, :]
            g_r = k_r * z_r - k_i * z_i
            g_i = k_r * z_i + k_i * z_r
            top_r = q_r * e_r - q_i * e_i
            top_i = q_r * e_i + q_i * e_r
            spectra[low, s * h : s * h + 128] = (g_r[:, :128] - top_i).astype(bf16)
            spectra[low, s * h + 128 : (s + 1) * h] = g_r[:, 128:].astype(bf16)
            spectra[high, s * h : s * h + 128] = (g_i[:, :128] + top_r).astype(bf16)
            spectra[high, s * h + 128 : (s + 1) * h] = g_i[:, 128:].astype(bf16)
        return carry

    lax.fori_loop(0, n // block, multiply, 0)

    for part in range(2):

        def write_columns(start, value, part=part):
            rows = pl.ds(start, value.shape[0])
            for s in range(2):
                columns[s, rows, part * h : (part + 1) * h] = value[:, s * h : (s + 1) * h].astype(bf16)

        blocked_dot(n, back_rows.at[part], spectra, write_columns)
    for s in range(2):

        def write_three(start, value, s=s):
            fields[2 + s, pl.ds(start, value.shape[0]), :] = value.astype(bf16)

        blocked_dot(n, columns.at[s], back_cols, write_three)
    send_strips(1)

    out[:, inner, :] = fields[:, inner, :].astype(f32)

    def ramps(shape, dim):
        steps = lax.broadcasted_iota(jnp.int32, shape, dim).astype(f32)
        return (steps + 0.5) * (1.0 / width), (width - 0.5 - steps) * (1.0 / width)

    for side, ramp in enumerate(ramps((1, width, 1), 1)):
        span = ends[side]

        @pl.when(has[side])
        def _():
            for pair in range(2):
                row_copy(1 - side, pair).wait_recv()
            out[:, span, :] = ramp * fields[:, span, :].astype(f32) + (1.0 - ramp) * from_rows[
                side
            ].astype(f32)

        @pl.when(jnp.logical_not(has[side]))
        def _():
            out[:, span, :] = fields[:, span, :].astype(f32)

        for other in range(2):
            corners[other, :, span, :] = out[:, span, ends[other]].astype(bf16)

            @pl.when(has[2 + other])
            def _():
                col_copy(other, side).start()

    for piece in (2, 3, 0, 1):
        part, span = (pl.ds(0, 4), ends[piece]) if piece < 2 else (pairs[piece - 2], inner)
        for side, ramp in enumerate(ramps((1, 1, width), 2)):

            @pl.when(has[2 + side])
            def _():
                col_copy(1 - side, piece).wait_recv()
                out[part, span, ends[side]] = ramp * out[part, span, ends[side]] + (
                    1.0 - ramp
                ) * from_cols[side, part, span, :].astype(f32)

    for side in range(2):

        @pl.when(has[side])
        def _():
            for pair in range(2):
                row_copy(side, pair).wait_send()

        @pl.when(has[2 + side])
        def _():
            for piece in range(4):
                col_copy(side, piece).wait_send()

    def finish(t, carry):
        o = place_of(t)

        @pl.when(o > 0)
        def _():
            for copy in copies(0, o):
                copy.wait_send()

        @pl.when(has_up)
        def _():
            for copy in copies(1, o):
                copy.wait_send()

        return carry

    lax.fori_loop(0, n_py, finish, 0)


def on_device(kappa, send_list, dest_slot, send_count):
    n_px = lax.axis_size("px")
    n_py = lax.axis_size("py")
    cap = send_list.shape[2]
    tile = kappa.shape[1]
    n = PATCH
    forward, down, back_rows, back_cols, slope, weights, edge = transform_tables(n)
    tables = [slope, forward, down, weights, edge, back_rows.reshape(2, n, 2 * n), back_cols]
    anywhere = pl.BlockSpec(memory_space=pl.ANY)
    vmem, bf16, f32 = pltpu.VMEM, jnp.bfloat16, jnp.float32
    dma = pltpu.SemaphoreType.DMA
    tiles, aux = (2, n_py, cap, tile), (2, n_py, 1, cap)
    return pl.pallas_call(
        functools.partial(flexion_kernel, n_px, n_py),
        out_shape=jax.ShapeDtypeStruct((4, n, n), f32),
        in_specs=[anywhere] * (4 + TABLES),
        out_specs=pl.BlockSpec(memory_space=vmem),
        scratch_shapes=[vmem(table.shape, table.dtype) for table in tables]
        + [
            vmem(kappa.shape, bf16),
            vmem(kappa.shape, f32),
            vmem((cap, tile), f32),
            vmem(tiles, bf16),
            vmem(aux, jnp.int32),
            vmem(tiles, bf16),
            vmem(aux, jnp.int32),
            pltpu.SMEM((2, n_py, cap), jnp.int32),
            vmem((2, n_py, cap), jnp.int32),
            pltpu.SMEM(send_count.shape, jnp.int32),
            vmem((n * n // tile, tile), f32),
            vmem((n, n), bf16),
            vmem((n, n), bf16),
            vmem((2 * n, n), f32),
            vmem((2 * n, n), bf16),
            vmem((2, n, n), bf16),
            vmem((4, n, n), bf16),
            vmem((2, 4, tile, n), bf16),
            vmem((2, 4, n, tile), bf16),
            vmem((2, 4, n, tile), bf16),
            dma((6 + TABLES,)),
        ]
        + [dma((2, n_py))] * 4
        + [dma((2, 2))] * 2
        + [dma((2, 4))] * 2,
        compiler_params=pltpu.CompilerParams(
            collective_id=0, has_side_effects=True, vmem_limit_bytes=58 * 2**20
        ),
        name="flexion",
    )(kappa, send_list, dest_slot, send_count, *tables)


def solution(mesh):
    placed = (
        P(("px", "py"), None),
        P(("px", "py"), None, None),
        P(("px", "py"), None, None),
        P(("px", "py"), None),
    )
    return jax.shard_map(
        on_device, mesh=mesh, in_specs=placed, out_specs=P(None, "px", "py"), check_vma=False
    )
```

```python
import functools
import math

import jax
import jax.numpy as jnp
import numpy as np
from jax import lax
from jax.experimental import pallas as pl
from jax.experimental.pallas import tpu as pltpu
from jax.sharding import PartitionSpec as P

PATCH = 512
MESH = pl.DeviceIdType.MESH
STEP = 16
PLACE = 512
RAISED = 128


def dft_tables(length):
    positions = np.arange(length)
    angles = (positions[:, None] * positions[None, :] % length).astype(np.float32) * np.float32(
        2.0 * math.pi / length
    )
    return np.cos(angles).astype(np.float32), np.sin(angles).astype(np.float32)


def wavenumbers(length):
    positions = np.arange(length)
    return (positions - length * (positions >= (length + 1) // 2)).astype(np.float32) * np.float32(2.0 / length)


def transform_tables(n):
    h = n // 2
    cos, sin = dft_tables(n)
    forward = np.concatenate([cos[:, :h], sin[:, :h]], 1)
    forward[:, h] = cos[:, h]
    back_cols = np.concatenate([2.0 * cos[:h], -2.0 * sin[:h]], 0)
    back_cols[0] = 1.0
    back_cols[h] = cos[h]
    signed = wavenumbers(n).astype(np.float64)
    order = np.arange(1, h)
    lag = np.arange(n)
    wave = -(2.0 / n) * (signed[1:h] * np.sin(2.0 * np.pi * (lag[:, None] * order % n) / n)).sum(1)
    slope = wave[(lag[None, :] - lag[:, None]) % n]
    return jnp.asarray(np.concatenate([slope, forward, back_cols, cos, sin], 0), jnp.bfloat16)


def blocked_dot(rows, left, right, write, block=256):
    def one(t, carry):
        start = pl.multiple_of(t * block, block)
        write(start, jnp.dot(left[pl.ds(start, block), :], right[...], preferred_element_type=jnp.float32))
        return carry

    lax.fori_loop(0, rows // block, one, 0)


def flexion_kernel(n_px, n_py, kappa, lists, slots, counts, *rest):
    source, out, table, back_rows, weights = rest[:5]
    slope, forward, back_cols = [table.at[pl.ds(k * PATCH, PATCH)] for k in range(3)]
    down = table.at[pl.ds(3 * PATCH, 2 * PATCH)]
    (
        held, wide, stage, tiles, aux, got_tiles, got_aux, rows, marks, totals, packed, bundle, bundle_to, far, far_to,
        patch, image, halves, spectrum, spectra, columns, fields, from_rows, from_cols, corners,
        load, send_t, recv_t, send_a, recv_a, send_v, recv_v, send_h, recv_h, send_b, recv_b,
    ) = rest[5:]
    i = lax.axis_index("px")
    j = lax.axis_index("py")
    cap = rows.shape[2]
    tile = wide.shape[1]
    n, h = PATCH, PATCH // 2
    slot_count = n * n // tile
    f32, bf16 = jnp.float32, jnp.bfloat16
    has_up, has_down = i > 0, i < n_px - 1
    upper = jnp.maximum(i - 1, 0)
    half = n_py // 2
    within = lax.rem(j, half)
    base_near = j - within
    partner = lax.rem(j + half, n_py)

    def near(r):
        return base_near + lax.rem(within + r, half)

    loads = [
        pltpu.make_async_copy(kappa, held, load.at[0]),
        pltpu.make_async_copy(counts, totals, load.at[1]),
    ]
    for b, band in enumerate((i, upper)):
        part = pl.ds(pl.multiple_of(band * n_py, n_py), n_py)
        loads.append(pltpu.make_async_copy(lists.at[0, part], rows.at[b], load.at[2 + b]))
        loads.append(pltpu.make_async_copy(slots.at[0, part], marks.at[b], load.at[4 + b]))
    table_load = pltpu.make_async_copy(source, table, load.at[6])
    for copy in loads:
        copy.start()

    barrier = pltpu.get_barrier_semaphore()
    for o in range(1, n_py):
        pl.semaphore_signal(barrier, inc=1, device_id=(i, lax.rem(j + o, n_py)), device_id_type=MESH)

    @pl.when(has_down)
    def _():
        for r in range(half):
            pl.semaphore_signal(barrier, inc=1, device_id=(i + 1, near(r)), device_id_type=MESH)

    @pl.when(has_up)
    def _():
        pl.semaphore_signal(barrier, inc=1, device_id=(i - 1, j), device_id_type=MESH)

    for copy in loads:
        copy.wait()
    table_load.start()
    wide[...] = held[...].astype(f32)
    patch[...] = jnp.zeros_like(patch)
    pl.semaphore_wait(
        barrier, n_py - 1 + jnp.where(has_up, half, 0) + jnp.where(has_down, 1, 0)
    )

    def copies(b, o):
        target = (i, lax.rem(j + o, n_py)) if b == 0 else (i - 1, near(lax.rem(o, half)))
        return [
            pltpu.make_async_remote_copy(
                src_ref=source.at[b, o],
                dst_ref=landing.at[b, o],
                send_sem=send.at[b, o],
                recv_sem=recv.at[b, o],
                device_id=target,
                device_id_type=MESH,
            )
            for source, landing, send, recv in (
                (tiles, got_tiles, send_t, recv_t),
                (aux, got_aux, send_a, recv_a),
            )
        ]

    lanes = lax.broadcasted_iota(jnp.int32, (1, cap), 1)

    def collect(b, o):
        if b == 0:
            column = lax.rem(j + o, n_py)
        else:
            column = lax.rem(near(lax.rem(o, half)) + half * (1 - o // half), n_py)

        def some(c, carry):
            base = pl.multiple_of(c * STEP, STEP)
            picks = [rows[b, column, base + k] for k in range(STEP)]
            values = [wide[pl.ds(pick, 1), :] for pick in picks]
            for k in range(STEP):
                stage[pl.ds(base + k, 1), :] = values[k]
            return carry

        lax.fori_loop(0, cap // STEP, some, 0)
        tiles[b, o] = stage[...].astype(bf16)
        count = totals[0, (i if b == 0 else upper) * n_py + column]
        aux[b, o] = jnp.where(lanes < count, marks[b, pl.ds(column, 1), :], slot_count)

    def place_of(t):
        step = (t + 1) // 2
        return lax.rem(n_py // 2 + step * (2 * lax.rem(t, 2) - 1) + n_py, n_py)

    def deliver(t, carry):
        o = place_of(t)
        collect(0, o)

        @pl.when(o > 0)
        def _():
            for copy in copies(0, o):
                copy.start()

        @pl.when(has_up)
        def _():
            collect(1, t)
            for copy in copies(1, t):
                copy.start()

        return carry

    lax.fori_loop(0, n_py, deliver, 0)

    table_load.wait()
    back_rows[0, :, :n] = table[3 * n : 4 * n, :]
    back_rows[0, :, n:] = -table[4 * n : 5 * n, :]
    back_rows[1, :, :n] = table[4 * n : 5 * n, :]
    back_rows[1, :, n:] = table[3 * n : 4 * n, :]
    block = 64

    def multipliers(t, carry):
        start = pl.multiple_of(t * block, block)
        row = lax.broadcasted_iota(jnp.int32, (block, h + 128), 0) + start
        col = lax.broadcasted_iota(jnp.int32, (block, h + 128), 1)
        along = (row - jnp.where(row >= h, n, 0)).astype(f32) * (2.0 / n)
        across = jnp.where(col < h, col, -h).astype(f32) * (2.0 / n)
        power = across * across + along * along
        scale = (1.0 / (n * n)) / jnp.where(power > 0, power, 1.0)
        scale = jnp.where(col <= h, scale, 0.0)
        weights[0, pl.ds(start, block), :] = (along * along - 3.0 * across * across) * along * scale
        weights[1, pl.ds(start, block), :] = (across * across - 3.0 * along * along) * across * scale
        return carry

    lax.fori_loop(0, n // block, multipliers, 0)

    def place(values, targets):
        def part(r, carry):
            base = pl.multiple_of(r * PLACE, PLACE)
            ids = lax.broadcasted_iota(jnp.int32, (PLACE, targets.shape[1]), 0) + base
            chosen = jnp.where(ids == targets, 1.0, 0.0).astype(bf16)
            patch[pl.ds(base, PLACE), :] += jnp.dot(chosen, values, preferred_element_type=f32)
            return carry

        lax.fori_loop(0, slot_count // PLACE, part, 0)

    raised = packed.shape[0]

    def bundle_copies():
        return [
            pltpu.make_async_remote_copy(
                src_ref=here,
                dst_ref=there,
                send_sem=send_b.at[k],
                recv_sem=recv_b.at[k],
                device_id=(i, partner),
                device_id_type=MESH,
            )
            for k, (here, there) in enumerate(((bundle, far), (bundle_to, far_to)))
        ]

    @pl.when(has_down)
    def _():
        packed[...] = jnp.zeros_like(packed)
        high_lane = lax.broadcasted_iota(jnp.int32, (8, cap), 0)

        def pack(r, carry):
            taken, digits = carry
            for copy in copies(1, r):
                copy.wait_recv()
            targets = got_aux[1, r]
            live = targets < slot_count
            position = jnp.where(live, taken + lanes, -1)
            ids = lax.broadcasted_iota(jnp.int32, (raised, cap), 0)
            chosen = jnp.where(ids == position, 1.0, 0.0).astype(bf16)
            packed[...] += jnp.dot(chosen, got_tiles[1, r], preferred_element_type=f32)
            parts = jnp.where(high_lane == 0, targets // 256, jnp.where(high_lane == 1, targets % 256, 1))
            digits += lax.dot_general(
                parts.astype(f32).astype(bf16), chosen, (((1,), (1,)), ((), ())), preferred_element_type=f32
            )
            return taken + jnp.sum(live.astype(jnp.int32), axis=1, keepdims=True), digits

        _, digits = lax.fori_loop(
            0, half, pack, (jnp.zeros((1, 1), jnp.int32), jnp.zeros((8, raised), f32))
        )
        digits = digits.astype(jnp.int32)
        bundle[...] = packed[...].astype(bf16)
        bundle_to[...] = jnp.where(digits[2:3] > 0, digits[0:1] * 256 + digits[1:2], slot_count)
        for copy in bundle_copies():
            copy.start()

    def receive(t, carry):
        o = place_of(t)

        @pl.when(o == 0)
        def _():
            place(tiles[0, 0], aux[0, 0])

        @pl.when(o > 0)
        def _():
            for copy in copies(0, o):
                copy.wait_recv()
            place(got_tiles[0, o], got_aux[0, o])

        @pl.when(jnp.logical_and(has_down, t >= half))
        def _():
            for copy in copies(1, t):
                copy.wait_recv()
            place(got_tiles[1, t], got_aux[1, t])

        return carry

    lax.fori_loop(0, n_py, receive, 0)

    @pl.when(has_down)
    def _():
        for copy in bundle_copies():
            copy.wait_recv()
        place(far[...], far_to[...])

    per_row = n // tile
    for c in range(per_row):
        image[:, c * tile : (c + 1) * tile] = patch[pl.ds(c, n, stride=per_row), :].astype(bf16)
    width = tile
    has = [has_up, has_down, j > 0, j < n_py - 1]
    beside = [(i - 1, j), (i + 1, j), (i, j - 1), (i, j + 1)]
    ends = [pl.ds(0, width), pl.ds(n - width, width)]
    inner = pl.ds(width, n - 2 * width)
    pairs = [pl.ds(0, 2), pl.ds(2, 2)]

    def row_copy(side, pair):
        return pltpu.make_async_remote_copy(
            src_ref=fields.at[pairs[pair], ends[side], :],
            dst_ref=from_rows.at[1 - side, pairs[pair]],
            send_sem=send_v.at[side, pair],
            recv_sem=recv_v.at[1 - side, pair],
            device_id=beside[side],
            device_id_type=MESH,
        )

    def col_copy(side, piece):
        if piece < 2:
            part, span = pl.ds(0, 4), ends[piece]
            source = corners.at[side, :, span, :]
        else:
            part, span = pairs[piece - 2], inner
            source = fields.at[part, inner, ends[side]]
        return pltpu.make_async_remote_copy(
            src_ref=source,
            dst_ref=from_cols.at[1 - side, part, span, :],
            send_sem=send_h.at[side, piece],
            recv_sem=recv_h.at[1 - side, piece],
            device_id=beside[2 + side],
            device_id_type=MESH,
        )

    def send_strips(pair):
        for side in range(2):

            @pl.when(has[side])
            def _():
                row_copy(side, pair).start()

            @pl.when(has[2 + side])
            def _():
                col_copy(side, 2 + pair).start()

    pixels = image[...].astype(f32)
    row_sign = 1.0 - 2.0 * (lax.broadcasted_iota(jnp.int32, (n, 1), 0) % 2).astype(f32)
    col_sign = 1.0 - 2.0 * (lax.broadcasted_iota(jnp.int32, (1, n), 1) % 2).astype(f32)
    row_edge = jnp.sum(pixels * row_sign, axis=0, keepdims=True) * (1.0 / n)

    def write_real(start, value):
        sign = 1.0 - 2.0 * (lax.broadcasted_iota(jnp.int32, (value.shape[0], 1), 0) % 2).astype(f32)
        fields[0, pl.ds(start, value.shape[0]), :] = (value + sign * row_edge).astype(bf16)

    def write_imag(start, value):
        own = image[pl.ds(start, value.shape[0]), :].astype(f32)
        col_edge = jnp.sum(own * col_sign, axis=1, keepdims=True) * (1.0 / n)
        fields[1, pl.ds(start, value.shape[0]), :] = (-value - col_edge * col_sign).astype(bf16)

    blocked_dot(n, image, slope, write_real)
    blocked_dot(n, slope, image, write_imag)
    send_strips(0)

    def write_halves(start, value):
        halves[pl.ds(start, value.shape[0]), :] = value.astype(bf16)

    def write_spectrum(start, value):
        spectrum[pl.ds(start, value.shape[0]), :] = value

    blocked_dot(n, image, forward, write_halves)
    blocked_dot(2 * n, down, halves, write_spectrum)

    first = lax.broadcasted_iota(jnp.int32, (1, h), 1) == 0

    def multiply(t, carry):
        start = pl.multiple_of(t * block, block)
        low = pl.ds(start, block)
        high = pl.ds(pl.multiple_of(start + n, block), block)
        z_r = spectrum[low, :h] - jnp.where(first, 0.0, spectrum[high, h:])
        z_i = -(spectrum[high, :h] + jnp.where(first, 0.0, spectrum[low, h:]))
        e_r = spectrum[low, h : h + 128]
        e_i = -spectrum[high, h : h + 128]
        k_r, k_i = weights[0, low, :h], weights[1, low, :h]
        q_r, q_i = weights[0, low, h:], weights[1, low, h:]
        last = lax.broadcasted_iota(jnp.int32, (block, 1), 0) + start == h
        r_last, r_rest = jnp.where(last, k_r, 0.0), jnp.where(last, 0.0, k_r)
        q_last, q_rest = jnp.where(last, q_r, 0.0), jnp.where(last, 0.0, q_r)
        parts = (
            (r_last * z_r - k_i * z_i, r_last * z_i + k_i * z_r, q_last * e_r, q_last * e_i),
            (r_rest * z_i, -r_rest * z_r, q_i * e_r + q_rest * e_i, q_i * e_i - q_rest * e_r),
        )
        for s, (g_r, g_i, top_r, top_i) in enumerate(parts):
            spectra[low, s * h : s * h + 128] = (g_r[:, :128] - top_i).astype(bf16)
            spectra[low, s * h + 128 : (s + 1) * h] = g_r[:, 128:].astype(bf16)
            spectra[high, s * h : s * h + 128] = (g_i[:, :128] + top_r).astype(bf16)
            spectra[high, s * h + 128 : (s + 1) * h] = g_i[:, 128:].astype(bf16)
        return carry

    lax.fori_loop(0, n // block, multiply, 0)

    for part in range(2):

        def write_columns(start, value, part=part):
            rows = pl.ds(start, value.shape[0])
            for s in range(2):
                columns[s, rows, part * h : (part + 1) * h] = value[:, s * h : (s + 1) * h].astype(bf16)

        blocked_dot(n, back_rows.at[part], spectra, write_columns)
    for s in range(2):

        def write_three(start, value, s=s):
            fields[2 + s, pl.ds(start, value.shape[0]), :] = value.astype(bf16)

        blocked_dot(n, columns.at[s], back_cols, write_three)
    send_strips(1)

    out[:, inner, :] = fields[:, inner, :]

    def ramps(shape, dim):
        steps = lax.broadcasted_iota(jnp.int32, shape, dim).astype(f32)
        return (steps + 0.5) * (1.0 / width), (width - 0.5 - steps) * (1.0 / width)

    for side, ramp in enumerate(ramps((1, width, 1), 1)):
        span = ends[side]

        @pl.when(has[side])
        def _():
            for pair in range(2):
                row_copy(1 - side, pair).wait_recv()
            own, other = fields[:, span, :].astype(f32), from_rows[side].astype(f32)
            out[:, span, :] = (ramp * own + (1.0 - ramp) * other).astype(bf16)

        @pl.when(jnp.logical_not(has[side]))
        def _():
            out[:, span, :] = fields[:, span, :]

        for other in range(2):
            corners[other, :, span, :] = out[:, span, ends[other]]

            @pl.when(has[2 + other])
            def _():
                col_copy(other, side).start()

    for piece in (2, 3, 0, 1):
        part, span = (pl.ds(0, 4), ends[piece]) if piece < 2 else (pairs[piece - 2], inner)
        for side, ramp in enumerate(ramps((1, 1, width), 2)):

            @pl.when(has[2 + side])
            def _():
                col_copy(1 - side, piece).wait_recv()
                own = out[part, span, ends[side]].astype(f32)
                other = from_cols[side, part, span, :].astype(f32)
                out[part, span, ends[side]] = (ramp * own + (1.0 - ramp) * other).astype(bf16)

    for side in range(2):

        @pl.when(has[side])
        def _():
            for pair in range(2):
                row_copy(side, pair).wait_send()

        @pl.when(has[2 + side])
        def _():
            for piece in range(4):
                col_copy(side, piece).wait_send()

    def finish(t, carry):
        o = place_of(t)

        @pl.when(o > 0)
        def _():
            for copy in copies(0, o):
                copy.wait_send()

        @pl.when(has_up)
        def _():
            for copy in copies(1, o):
                copy.wait_send()

        return carry

    lax.fori_loop(0, n_py, finish, 0)

    @pl.when(has_down)
    def _():
        for copy in bundle_copies():
            copy.wait_send()


def on_device(kappa, send_list, dest_slot, send_count):
    n_px = lax.axis_size("px")
    n_py = lax.axis_size("py")
    cap = send_list.shape[2]
    tile = kappa.shape[1]
    n = PATCH
    raised = RAISED * n // tile
    anywhere = pl.BlockSpec(memory_space=pl.ANY)
    vmem, bf16, f32 = pltpu.VMEM, jnp.bfloat16, jnp.float32
    dma = pltpu.SemaphoreType.DMA
    tiles, aux = (2, n_py, cap, tile), (2, n_py, 1, cap)
    blended = pl.pallas_call(
        functools.partial(flexion_kernel, n_px, n_py),
        out_shape=jax.ShapeDtypeStruct((4, n, n), bf16),
        in_specs=[anywhere] * 5,
        out_specs=pl.BlockSpec(memory_space=vmem),
        scratch_shapes=[
            vmem((5 * n, n), bf16),
            vmem((2, n, 2 * n), bf16),
            vmem((2, n, n // 2 + 128), f32),
            vmem(kappa.shape, bf16),
            vmem(kappa.shape, f32),
            vmem((cap, tile), f32),
            vmem(tiles, bf16),
            vmem(aux, jnp.int32),
            vmem(tiles, bf16),
            vmem(aux, jnp.int32),
            pltpu.SMEM((2, n_py, cap), jnp.int32),
            vmem((2, n_py, cap), jnp.int32),
            pltpu.SMEM(send_count.shape, jnp.int32),
            vmem((raised, tile), f32),
            vmem((raised, tile), bf16),
            vmem((1, raised), jnp.int32),
            vmem((raised, tile), bf16),
            vmem((1, raised), jnp.int32),
            vmem((n * n // tile, tile), f32),
            vmem((n, n), bf16),
            vmem((n, n), bf16),
            vmem((2 * n, n), f32),
            vmem((2 * n, n), bf16),
            vmem((2, n, n), bf16),
            vmem((4, n, n), bf16),
            vmem((2, 4, tile, n), bf16),
            vmem((2, 4, n, tile), bf16),
            vmem((2, 4, n, tile), bf16),
            dma((7,)),
        ]
        + [dma((2, n_py))] * 4
        + [dma((2, 2))] * 2
        + [dma((2, 4))] * 2
        + [dma((2,))] * 2,
        compiler_params=pltpu.CompilerParams(
            collective_id=0, has_side_effects=True, vmem_limit_bytes=58 * 2**20
        ),
        name="flexion",
    )(kappa, send_list, dest_slot, send_count, transform_tables(n))
    return blended.astype(f32)


def solution(mesh):
    placed = (
        P(("px", "py"), None),
        P(("px", "py"), None, None),
        P(("px", "py"), None, None),
        P(("px", "py"), None),
    )
    return jax.shard_map(
        on_device, mesh=mesh, in_specs=placed, out_specs=P(None, "px", "py"), check_vma=False
    )
```

```python
import functools
import math

import jax
import jax.numpy as jnp
import numpy as np
from jax import lax
from jax.experimental import pallas as pl
from jax.experimental.pallas import tpu as pltpu
from jax.sharding import PartitionSpec as P

PATCH = 512
MESH = pl.DeviceIdType.MESH
STEP = 16
RAISED = 128


def dft_tables(length):
    positions = np.arange(length)
    angles = (positions[:, None] * positions[None, :] % length).astype(np.float32) * np.float32(
        2.0 * math.pi / length
    )
    return np.cos(angles).astype(np.float32), np.sin(angles).astype(np.float32)


def wavenumbers(length):
    positions = np.arange(length)
    return (positions - length * (positions >= (length + 1) // 2)).astype(np.float32) * np.float32(2.0 / length)


def transform_tables(n):
    h = n // 2
    cos, sin = dft_tables(n)
    forward = np.concatenate([cos[:, :h], sin[:, :h]], 1)
    forward[:, h] = cos[:, h]
    back_cols = np.concatenate([2.0 * cos[:h], -2.0 * sin[:h]], 0)
    back_cols[0] = 1.0
    back_cols[h] = cos[h]
    signed = wavenumbers(n).astype(np.float64)
    order = np.arange(1, h)
    lag = np.arange(n)
    wave = -(2.0 / n) * (signed[1:h] * np.sin(2.0 * np.pi * (lag[:, None] * order % n) / n)).sum(1)
    slope = wave[(lag[None, :] - lag[:, None]) % n]
    return jnp.asarray(np.concatenate([slope, forward, back_cols, cos, sin], 0), jnp.bfloat16)


def blocked_dot(rows, left, right, write, block=256):
    def one(t, carry):
        start = pl.multiple_of(t * block, block)
        write(start, jnp.dot(left[pl.ds(start, block), :], right[...], preferred_element_type=jnp.float32))
        return carry

    lax.fori_loop(0, rows // block, one, 0)


def flexion_kernel(n_px, n_py, kappa, lists, slots, counts, *rest):
    source, out, table, back_rows, weights = rest[:5]
    slope, forward, back_cols = [table.at[pl.ds(k * PATCH, PATCH)] for k in range(3)]
    down = table.at[pl.ds(3 * PATCH, 2 * PATCH)]
    (
        held, wide, stage, tiles, aux, got_tiles, got_aux, rows, marks, totals, packed, bundle, bundle_to, far, far_to,
        patch, image, halves, spectrum, spectra, columns, fields, from_rows, from_cols, corners,
        load, send_t, recv_t, send_a, recv_a, send_v, recv_v, send_h, recv_h, send_b, recv_b,
    ) = rest[5:]
    i = lax.axis_index("px")
    j = lax.axis_index("py")
    cap = rows.shape[2]
    tile = wide.shape[1]
    n, h = PATCH, PATCH // 2
    slot_count = n * n // tile
    f32, bf16 = jnp.float32, jnp.bfloat16
    has_up, has_down = i > 0, i < n_px - 1
    upper = jnp.maximum(i - 1, 0)
    half = n_py // 2
    within = lax.rem(j, half)
    base_near = j - within
    partner = lax.rem(j + half, n_py)

    def near(r):
        return base_near + lax.rem(within + r, half)

    loads = [
        pltpu.make_async_copy(kappa, held, load.at[0]),
        pltpu.make_async_copy(counts, totals, load.at[1]),
    ]
    for b, band in enumerate((i, upper)):
        part = pl.ds(pl.multiple_of(band * n_py, n_py), n_py)
        loads.append(pltpu.make_async_copy(lists.at[0, part], rows.at[b], load.at[2 + b]))
        loads.append(pltpu.make_async_copy(slots.at[0, part], marks.at[b], load.at[4 + b]))
    table_load = pltpu.make_async_copy(source, table, load.at[6])
    for copy in loads:
        copy.start()

    barrier = pltpu.get_barrier_semaphore()
    for o in range(1, n_py):
        pl.semaphore_signal(barrier, inc=1, device_id=(i, lax.rem(j + o, n_py)), device_id_type=MESH)

    @pl.when(has_down)
    def _():
        for r in range(half):
            pl.semaphore_signal(barrier, inc=1, device_id=(i + 1, near(r)), device_id_type=MESH)

    @pl.when(has_up)
    def _():
        pl.semaphore_signal(barrier, inc=1, device_id=(i - 1, j), device_id_type=MESH)

    for copy in loads:
        copy.wait()
    table_load.start()
    wide[...] = held[...].astype(f32)
    patch[...] = jnp.zeros_like(patch)
    pl.semaphore_wait(
        barrier, n_py - 1 + jnp.where(has_up, half, 0) + jnp.where(has_down, 1, 0)
    )

    def copies(b, o):
        target = (i, lax.rem(j + o, n_py)) if b == 0 else (i - 1, near(lax.rem(o, half)))
        return [
            pltpu.make_async_remote_copy(
                src_ref=source.at[b, o],
                dst_ref=landing.at[b, o],
                send_sem=send.at[b, o],
                recv_sem=recv.at[b, o],
                device_id=target,
                device_id_type=MESH,
            )
            for source, landing, send, recv in (
                (tiles, got_tiles, send_t, recv_t),
                (aux, got_aux, send_a, recv_a),
            )
        ]

    lanes = lax.broadcasted_iota(jnp.int32, (1, cap), 1)

    def collect(b, o):
        if b == 0:
            column = lax.rem(j + o, n_py)
        else:
            column = lax.rem(near(lax.rem(o, half)) + half * (1 - o // half), n_py)

        def some(c, carry):
            base = pl.multiple_of(c * STEP, STEP)
            picks = [rows[b, column, base + k] for k in range(STEP)]
            values = [wide[pl.ds(pick, 1), :] for pick in picks]
            for k in range(STEP):
                stage[pl.ds(base + k, 1), :] = values[k]
            return carry

        lax.fori_loop(0, cap // STEP, some, 0)
        tiles[b, o] = stage[...].astype(bf16)
        count = totals[0, (i if b == 0 else upper) * n_py + column]
        aux[b, o] = jnp.where(lanes < count, marks[b, pl.ds(column, 1), :], slot_count)

    def place_of(t):
        step = (t + 1) // 2
        return lax.rem(n_py // 2 + step * (2 * lax.rem(t, 2) - 1) + n_py, n_py)

    def deliver(t, carry):
        o = place_of(t)
        collect(0, o)

        @pl.when(o > 0)
        def _():
            for copy in copies(0, o):
                copy.start()

        @pl.when(has_up)
        def _():
            collect(1, t)
            for copy in copies(1, t):
                copy.start()

        return carry

    lax.fori_loop(0, n_py, deliver, 0)

    table_load.wait()
    back_rows[0, :, :n] = table[3 * n : 4 * n, :]
    back_rows[0, :, n:] = -table[4 * n : 5 * n, :]
    back_rows[1, :, :n] = table[4 * n : 5 * n, :]
    back_rows[1, :, n:] = table[3 * n : 4 * n, :]
    block = 64

    def multipliers(t, carry):
        start = pl.multiple_of(t * block, block)
        row = lax.broadcasted_iota(jnp.int32, (block, h + 128), 0) + start
        col = lax.broadcasted_iota(jnp.int32, (block, h + 128), 1)
        along = (row - jnp.where(row >= h, n, 0)).astype(f32) * (2.0 / n)
        across = jnp.where(col < h, col, -h).astype(f32) * (2.0 / n)
        power = across * across + along * along
        scale = (1.0 / (n * n)) / jnp.where(power > 0, power, 1.0)
        scale = jnp.where(col <= h, scale, 0.0)
        weights[0, pl.ds(start, block), :] = (along * along - 3.0 * across * across) * along * scale
        weights[1, pl.ds(start, block), :] = (across * across - 3.0 * along * along) * across * scale
        return carry

    lax.fori_loop(0, n // block, multipliers, 0)

    per_row = n // tile

    def place(values, targets):
        count = targets.shape[1]
        ids = lax.broadcasted_iota(jnp.int32, (n, count), 0)
        chosen = jnp.where(ids == targets // per_row, 1.0, 0.0).astype(bf16)
        block_of = jnp.transpose(jnp.broadcast_to(targets % per_row, (8, count)))[:, :1]
        spread = jnp.concatenate(
            [jnp.where(block_of == c, values, jnp.zeros_like(values)) for c in range(per_row)], axis=1
        )
        patch[...] += jnp.dot(chosen, spread, preferred_element_type=f32)

    raised = packed.shape[0]

    def bundle_copies():
        return [
            pltpu.make_async_remote_copy(
                src_ref=here,
                dst_ref=there,
                send_sem=send_b.at[k],
                recv_sem=recv_b.at[k],
                device_id=(i, partner),
                device_id_type=MESH,
            )
            for k, (here, there) in enumerate(((bundle, far), (bundle_to, far_to)))
        ]

    @pl.when(has_down)
    def _():
        packed[...] = jnp.zeros_like(packed)
        high_lane = lax.broadcasted_iota(jnp.int32, (8, cap), 0)

        def pack(r, carry):
            taken, digits = carry
            for copy in copies(1, r):
                copy.wait_recv()
            targets = got_aux[1, r]
            live = targets < slot_count
            position = jnp.where(live, taken + lanes, -1)
            ids = lax.broadcasted_iota(jnp.int32, (raised, cap), 0)
            chosen = jnp.where(ids == position, 1.0, 0.0).astype(bf16)
            packed[...] += jnp.dot(chosen, got_tiles[1, r], preferred_element_type=f32)
            parts = jnp.where(high_lane == 0, targets // 256, jnp.where(high_lane == 1, targets % 256, 1))
            digits += lax.dot_general(
                parts.astype(f32).astype(bf16), chosen, (((1,), (1,)), ((), ())), preferred_element_type=f32
            )
            return taken + jnp.sum(live.astype(jnp.int32), axis=1, keepdims=True), digits

        _, digits = lax.fori_loop(
            0, half, pack, (jnp.zeros((1, 1), jnp.int32), jnp.zeros((8, raised), f32))
        )
        digits = digits.astype(jnp.int32)
        bundle[...] = packed[...].astype(bf16)
        bundle_to[...] = jnp.where(digits[2:3] > 0, digits[0:1] * 256 + digits[1:2], slot_count)
        for copy in bundle_copies():
            copy.start()

    def two(b, a, c):
        place(
            jnp.concatenate([got_tiles[b, a], got_tiles[b, c]], axis=0),
            jnp.concatenate([got_aux[b, a], got_aux[b, c]], axis=1),
        )

    def receive(u, carry):
        first, second = place_of(2 * u), place_of(2 * u + 1)
        for copy in copies(0, first):
            copy.wait_recv()

        @pl.when(second > 0)
        def _():
            for copy in copies(0, second):
                copy.wait_recv()

        @pl.when(second == 0)
        def _():
            got_tiles[0, 0] = tiles[0, 0]
            got_aux[0, 0] = aux[0, 0]

        two(0, first, second)

        @pl.when(jnp.logical_and(has_down, 2 * u >= half))
        def _():
            for t in (2 * u, 2 * u + 1):
                for copy in copies(1, t):
                    copy.wait_recv()
            two(1, 2 * u, 2 * u + 1)

        return carry

    lax.fori_loop(0, half, receive, 0)

    @pl.when(has_down)
    def _():
        for copy in bundle_copies():
            copy.wait_recv()
        place(far[...], far_to[...])

    image[...] = patch[...].astype(bf16)

    width = tile
    has = [has_up, has_down, j > 0, j < n_py - 1]
    beside = [(i - 1, j), (i + 1, j), (i, j - 1), (i, j + 1)]
    ends = [pl.ds(0, width), pl.ds(n - width, width)]
    inner = pl.ds(width, n - 2 * width)
    pairs = [pl.ds(0, 2), pl.ds(2, 2)]

    def row_copy(side, pair):
        return pltpu.make_async_remote_copy(
            src_ref=fields.at[pairs[pair], ends[side], :],
            dst_ref=from_rows.at[1 - side, pairs[pair]],
            send_sem=send_v.at[side, pair],
            recv_sem=recv_v.at[1 - side, pair],
            device_id=beside[side],
            device_id_type=MESH,
        )

    def col_copy(side, piece):
        if piece < 2:
            part, span = pl.ds(0, 4), ends[piece]
            source = corners.at[side, :, span, :]
        else:
            part, span = pairs[piece - 2], inner
            source = fields.at[part, inner, ends[side]]
        return pltpu.make_async_remote_copy(
            src_ref=source,
            dst_ref=from_cols.at[1 - side, part, span, :],
            send_sem=send_h.at[side, piece],
            recv_sem=recv_h.at[1 - side, piece],
            device_id=beside[2 + side],
            device_id_type=MESH,
        )

    def send_strips(pair):
        for side in range(2):

            @pl.when(has[side])
            def _():
                row_copy(side, pair).start()

            @pl.when(has[2 + side])
            def _():
                col_copy(side, 2 + pair).start()

    pixels = image[...].astype(f32)
    row_sign = 1.0 - 2.0 * (lax.broadcasted_iota(jnp.int32, (n, 1), 0) % 2).astype(f32)
    col_sign = 1.0 - 2.0 * (lax.broadcasted_iota(jnp.int32, (1, n), 1) % 2).astype(f32)
    row_edge = jnp.sum(pixels * row_sign, axis=0, keepdims=True) * (1.0 / n)

    def write_real(start, value):
        sign = 1.0 - 2.0 * (lax.broadcasted_iota(jnp.int32, (value.shape[0], 1), 0) % 2).astype(f32)
        fields[0, pl.ds(start, value.shape[0]), :] = (value + sign * row_edge).astype(bf16)

    def write_imag(start, value):
        own = image[pl.ds(start, value.shape[0]), :].astype(f32)
        col_edge = jnp.sum(own * col_sign, axis=1, keepdims=True) * (1.0 / n)
        fields[1, pl.ds(start, value.shape[0]), :] = (-value - col_edge * col_sign).astype(bf16)

    blocked_dot(n, image, slope, write_real)
    blocked_dot(n, slope, image, write_imag)
    send_strips(0)

    def write_halves(start, value):
        halves[pl.ds(start, value.shape[0]), :] = value.astype(bf16)

    def write_spectrum(start, value):
        spectrum[pl.ds(start, value.shape[0]), :] = value

    blocked_dot(n, image, forward, write_halves)
    blocked_dot(2 * n, down, halves, write_spectrum)

    first = lax.broadcasted_iota(jnp.int32, (1, h), 1) == 0

    def multiply(t, carry):
        start = pl.multiple_of(t * block, block)
        low = pl.ds(start, block)
        high = pl.ds(pl.multiple_of(start + n, block), block)
        z_r = spectrum[low, :h] - jnp.where(first, 0.0, spectrum[high, h:])
        z_i = -(spectrum[high, :h] + jnp.where(first, 0.0, spectrum[low, h:]))
        e_r = spectrum[low, h : h + 128]
        e_i = -spectrum[high, h : h + 128]
        k_r, k_i = weights[0, low, :h], weights[1, low, :h]
        q_r, q_i = weights[0, low, h:], weights[1, low, h:]
        last = lax.broadcasted_iota(jnp.int32, (block, 1), 0) + start == h
        r_last, r_rest = jnp.where(last, k_r, 0.0), jnp.where(last, 0.0, k_r)
        q_last, q_rest = jnp.where(last, q_r, 0.0), jnp.where(last, 0.0, q_r)
        parts = (
            (r_last * z_r - k_i * z_i, r_last * z_i + k_i * z_r, q_last * e_r, q_last * e_i),
            (r_rest * z_i, -r_rest * z_r, q_i * e_r + q_rest * e_i, q_i * e_i - q_rest * e_r),
        )
        for s, (g_r, g_i, top_r, top_i) in enumerate(parts):
            spectra[low, s * h : s * h + 128] = (g_r[:, :128] - top_i).astype(bf16)
            spectra[low, s * h + 128 : (s + 1) * h] = g_r[:, 128:].astype(bf16)
            spectra[high, s * h : s * h + 128] = (g_i[:, :128] + top_r).astype(bf16)
            spectra[high, s * h + 128 : (s + 1) * h] = g_i[:, 128:].astype(bf16)
        return carry

    lax.fori_loop(0, n // block, multiply, 0)

    for part in range(2):

        def write_columns(start, value, part=part):
            rows = pl.ds(start, value.shape[0])
            for s in range(2):
                columns[s, rows, part * h : (part + 1) * h] = value[:, s * h : (s + 1) * h].astype(bf16)

        blocked_dot(n, back_rows.at[part], spectra, write_columns)
    for s in range(2):

        def write_three(start, value, s=s):
            fields[2 + s, pl.ds(start, value.shape[0]), :] = value.astype(bf16)

        blocked_dot(n, columns.at[s], back_cols, write_three)
    send_strips(1)

    out[:, inner, :] = fields[:, inner, :]

    def ramps(shape, dim):
        steps = lax.broadcasted_iota(jnp.int32, shape, dim).astype(f32)
        return (steps + 0.5) * (1.0 / width), (width - 0.5 - steps) * (1.0 / width)

    for side, ramp in enumerate(ramps((1, width, 1), 1)):
        span = ends[side]

        @pl.when(has[side])
        def _():
            for pair in range(2):
                row_copy(1 - side, pair).wait_recv()
            own, other = fields[:, span, :].astype(f32), from_rows[side].astype(f32)
            out[:, span, :] = (ramp * own + (1.0 - ramp) * other).astype(bf16)

        @pl.when(jnp.logical_not(has[side]))
        def _():
            out[:, span, :] = fields[:, span, :]

        for other in range(2):
            corners[other, :, span, :] = out[:, span, ends[other]]

            @pl.when(has[2 + other])
            def _():
                col_copy(other, side).start()

    for piece in (2, 3, 0, 1):
        part, span = (pl.ds(0, 4), ends[piece]) if piece < 2 else (pairs[piece - 2], inner)
        for side, ramp in enumerate(ramps((1, 1, width), 2)):

            @pl.when(has[2 + side])
            def _():
                col_copy(1 - side, piece).wait_recv()
                own = out[part, span, ends[side]].astype(f32)
                other = from_cols[side, part, span, :].astype(f32)
                out[part, span, ends[side]] = (ramp * own + (1.0 - ramp) * other).astype(bf16)

    for side in range(2):

        @pl.when(has[side])
        def _():
            for pair in range(2):
                row_copy(side, pair).wait_send()

        @pl.when(has[2 + side])
        def _():
            for piece in range(4):
                col_copy(side, piece).wait_send()

    def finish(t, carry):
        o = place_of(t)

        @pl.when(o > 0)
        def _():
            for copy in copies(0, o):
                copy.wait_send()

        @pl.when(has_up)
        def _():
            for copy in copies(1, o):
                copy.wait_send()

        return carry

    lax.fori_loop(0, n_py, finish, 0)

    @pl.when(has_down)
    def _():
        for copy in bundle_copies():
            copy.wait_send()


def widen_kernel(narrow, out):
    out[...] = narrow[...].astype(jnp.float32)


def on_device(kappa, send_list, dest_slot, send_count):
    n_px = lax.axis_size("px")
    n_py = lax.axis_size("py")
    cap = send_list.shape[2]
    tile = kappa.shape[1]
    n = PATCH
    raised = RAISED * n // tile
    anywhere = pl.BlockSpec(memory_space=pl.ANY)
    vmem, bf16, f32 = pltpu.VMEM, jnp.bfloat16, jnp.float32
    dma = pltpu.SemaphoreType.DMA
    tiles, aux = (2, n_py, cap, tile), (2, n_py, 1, cap)
    blended = pl.pallas_call(
        functools.partial(flexion_kernel, n_px, n_py),
        out_shape=jax.ShapeDtypeStruct((4, n, n), bf16),
        in_specs=[anywhere] * 5,
        out_specs=pl.BlockSpec(memory_space=vmem),
        scratch_shapes=[
            vmem((5 * n, n), bf16),
            vmem((2, n, 2 * n), bf16),
            vmem((2, n, n // 2 + 128), f32),
            vmem(kappa.shape, bf16),
            vmem(kappa.shape, f32),
            vmem((cap, tile), f32),
            vmem(tiles, bf16),
            vmem(aux, jnp.int32),
            vmem(tiles, bf16),
            vmem(aux, jnp.int32),
            pltpu.SMEM((2, n_py, cap), jnp.int32),
            vmem((2, n_py, cap), jnp.int32),
            pltpu.SMEM(send_count.shape, jnp.int32),
            vmem((raised, tile), f32),
            vmem((raised, tile), bf16),
            vmem((1, raised), jnp.int32),
            vmem((raised, tile), bf16),
            vmem((1, raised), jnp.int32),
            vmem((n, n), f32),
            vmem((n, n), bf16),
            vmem((n, n), bf16),
            vmem((2 * n, n), f32),
            vmem((2 * n, n), bf16),
            vmem((2, n, n), bf16),
            vmem((4, n, n), bf16),
            vmem((2, 4, tile, n), bf16),
            vmem((2, 4, n, tile), bf16),
            vmem((2, 4, n, tile), bf16),
            dma((7,)),
        ]
        + [dma((2, n_py))] * 4
        + [dma((2, 2))] * 2
        + [dma((2, 4))] * 2
        + [dma((2,))] * 2,
        compiler_params=pltpu.CompilerParams(
            collective_id=0, has_side_effects=True, vmem_limit_bytes=58 * 2**20
        ),
        name="flexion",
    )(kappa, send_list, dest_slot, send_count, transform_tables(n))
    block = pl.BlockSpec((1, n // 2, n), lambda k, r: (k, r, 0))
    return pl.pallas_call(
        widen_kernel,
        out_shape=jax.ShapeDtypeStruct((4, n, n), f32),
        grid=(4, 2),
        in_specs=[block],
        out_specs=block,
        name="widen",
    )(blended)


def solution(mesh):
    placed = (
        P(("px", "py"), None),
        P(("px", "py"), None, None),
        P(("px", "py"), None, None),
        P(("px", "py"), None),
    )
    return jax.shard_map(
        on_device, mesh=mesh, in_specs=placed, out_specs=P(None, "px", "py"), check_vma=False
    )
```

```python
import functools
import math

import jax
import jax.numpy as jnp
import numpy as np
from jax import lax
from jax.experimental import pallas as pl
from jax.experimental.pallas import tpu as pltpu
from jax.sharding import PartitionSpec as P

PATCH = 512
MESH = pl.DeviceIdType.MESH
STEP = 16
RAISED = 128


def dft_tables(length):
    positions = np.arange(length)
    angles = (positions[:, None] * positions[None, :] % length).astype(np.float32) * np.float32(
        2.0 * math.pi / length
    )
    return np.cos(angles).astype(np.float32), np.sin(angles).astype(np.float32)


def wavenumbers(length):
    positions = np.arange(length)
    return (positions - length * (positions >= (length + 1) // 2)).astype(np.float32) * np.float32(2.0 / length)


def transform_tables(n):
    h = n // 2
    cos, sin = dft_tables(n)
    forward = np.concatenate([cos[:, :h], sin[:, :h]], 1)
    forward[:, h] = cos[:, h]
    back_cols = np.concatenate([2.0 * cos[:h], -2.0 * sin[:h]], 0)
    back_cols[0] = 1.0
    back_cols[h] = cos[h]
    signed = wavenumbers(n).astype(np.float64)
    order = np.arange(1, h)
    lag = np.arange(n)
    wave = -(2.0 / n) * (signed[1:h] * np.sin(2.0 * np.pi * (lag[:, None] * order % n) / n)).sum(1)
    slope = wave[(lag[None, :] - lag[:, None]) % n]
    return jnp.asarray(np.concatenate([slope, forward, back_cols, cos, sin], 0), jnp.bfloat16)


def blocked_dot(rows, left, right, write, block=256):
    def one(t, carry):
        start = pl.multiple_of(t * block, block)
        write(start, jnp.dot(left[pl.ds(start, block), :], right[...], preferred_element_type=jnp.float32))
        return carry

    lax.fori_loop(0, rows // block, one, 0)


def flexion_kernel(n_px, n_py, kappa, lists, slots, counts, *rest):
    source, out, table, back_rows, weights = rest[:5]
    slope, forward, back_cols = [table.at[pl.ds(k * PATCH, PATCH)] for k in range(3)]
    down = table.at[pl.ds(3 * PATCH, 2 * PATCH)]
    (
        held, wide, stage, tiles, aux, got_tiles, got_aux, rows, marks, totals, packed, bundle, bundle_to, far, far_to,
        patch, image, halves, spectrum, spectra, columns, fields, from_rows, from_cols, corners,
        load, send_t, recv_t, send_a, recv_a, send_v, recv_v, send_h, recv_h, send_b, recv_b,
    ) = rest[5:]
    i = lax.axis_index("px")
    j = lax.axis_index("py")
    cap = rows.shape[2]
    tile = wide.shape[1]
    n, h = PATCH, PATCH // 2
    slot_count = n * n // tile
    f32, bf16 = jnp.float32, jnp.bfloat16
    has_up, has_down = i > 0, i < n_px - 1
    upper = jnp.maximum(i - 1, 0)
    half = n_py // 2
    within = lax.rem(j, half)
    base_near = j - within
    partner = lax.rem(j + half, n_py)

    def near(r):
        return base_near + lax.rem(within + r, half)

    loads = [
        pltpu.make_async_copy(kappa, held, load.at[0]),
        pltpu.make_async_copy(counts, totals, load.at[1]),
    ]
    for b, band in enumerate((i, upper)):
        part = pl.ds(pl.multiple_of(band * n_py, n_py), n_py)
        loads.append(pltpu.make_async_copy(lists.at[0, part], rows.at[b], load.at[2 + b]))
        loads.append(pltpu.make_async_copy(slots.at[0, part], marks.at[b], load.at[4 + b]))
    table_load = pltpu.make_async_copy(source, table, load.at[6])
    for copy in loads:
        copy.start()

    barrier = pltpu.get_barrier_semaphore()
    for o in range(1, n_py):
        pl.semaphore_signal(barrier, inc=1, device_id=(i, lax.rem(j + o, n_py)), device_id_type=MESH)

    @pl.when(has_down)
    def _():
        for r in range(half):
            pl.semaphore_signal(barrier, inc=1, device_id=(i + 1, near(r)), device_id_type=MESH)

    @pl.when(has_up)
    def _():
        pl.semaphore_signal(barrier, inc=1, device_id=(i - 1, j), device_id_type=MESH)

    for copy in loads:
        copy.wait()
    table_load.start()
    wide[...] = held[...].astype(f32)
    patch[...] = jnp.zeros_like(patch)
    pl.semaphore_wait(
        barrier, n_py - 1 + jnp.where(has_up, half, 0) + jnp.where(has_down, 1, 0)
    )

    def copies(b, o):
        target = (i, lax.rem(j + o, n_py)) if b == 0 else (i - 1, near(lax.rem(o, half)))
        return [
            pltpu.make_async_remote_copy(
                src_ref=source.at[b, o],
                dst_ref=landing.at[b, o],
                send_sem=send.at[b, o],
                recv_sem=recv.at[b, o],
                device_id=target,
                device_id_type=MESH,
            )
            for source, landing, send, recv in (
                (tiles, got_tiles, send_t, recv_t),
                (aux, got_aux, send_a, recv_a),
            )
        ]

    lanes = lax.broadcasted_iota(jnp.int32, (1, cap), 1)

    def collect(b, o):
        if b == 0:
            column = lax.rem(j + o, n_py)
        else:
            column = lax.rem(near(lax.rem(o, half)) + half * (1 - o // half), n_py)

        def some(c, carry):
            base = pl.multiple_of(c * STEP, STEP)
            picks = [rows[b, column, base + k] for k in range(STEP)]
            values = [wide[pl.ds(pick, 1), :] for pick in picks]
            for k in range(STEP):
                stage[pl.ds(base + k, 1), :] = values[k]
            return carry

        lax.fori_loop(0, cap // STEP, some, 0)
        tiles[b, o] = stage[...].astype(bf16)
        count = totals[0, (i if b == 0 else upper) * n_py + column]
        aux[b, o] = jnp.where(lanes < count, marks[b, pl.ds(column, 1), :], slot_count)

    def place_of(t):
        step = (t + 1) // 2
        return lax.rem(n_py // 2 + step * (2 * lax.rem(t, 2) - 1) + n_py, n_py)

    def deliver(t, carry):
        o = place_of(t)
        collect(0, o)

        @pl.when(o > 0)
        def _():
            for copy in copies(0, o):
                copy.start()

        @pl.when(has_up)
        def _():
            collect(1, t)
            for copy in copies(1, t):
                copy.start()

        return carry

    lax.fori_loop(0, n_py, deliver, 0)


    per_row = n // tile

    def place(values, targets):
        count = targets.shape[1]
        ids = lax.broadcasted_iota(jnp.int32, (n, count), 0)
        chosen = jnp.where(ids == targets // per_row, 1.0, 0.0).astype(bf16)
        block_of = jnp.transpose(jnp.broadcast_to(targets % per_row, (8, count)))[:, :1]
        spread = jnp.concatenate(
            [jnp.where(block_of == c, values, jnp.zeros_like(values)) for c in range(per_row)], axis=1
        )
        patch[...] += jnp.dot(chosen, spread, preferred_element_type=f32)

    raised = packed.shape[0]

    def bundle_copies():
        return [
            pltpu.make_async_remote_copy(
                src_ref=here,
                dst_ref=there,
                send_sem=send_b.at[k],
                recv_sem=recv_b.at[k],
                device_id=(i, partner),
                device_id_type=MESH,
            )
            for k, (here, there) in enumerate(((bundle, far), (bundle_to, far_to)))
        ]

    @pl.when(has_down)
    def _():
        packed[...] = jnp.zeros_like(packed)
        high_lane = lax.broadcasted_iota(jnp.int32, (8, cap), 0)

        def pack(r, carry):
            taken, digits = carry
            for copy in copies(1, r):
                copy.wait_recv()
            targets = got_aux[1, r]
            live = targets < slot_count
            position = jnp.where(live, taken + lanes, -1)
            ids = lax.broadcasted_iota(jnp.int32, (raised, cap), 0)
            chosen = jnp.where(ids == position, 1.0, 0.0).astype(bf16)
            packed[...] += jnp.dot(chosen, got_tiles[1, r], preferred_element_type=f32)
            parts = jnp.where(high_lane == 0, targets // 256, jnp.where(high_lane == 1, targets % 256, 1))
            digits += lax.dot_general(
                parts.astype(f32).astype(bf16), chosen, (((1,), (1,)), ((), ())), preferred_element_type=f32
            )
            return taken + jnp.sum(live.astype(jnp.int32), axis=1, keepdims=True), digits

        _, digits = lax.fori_loop(
            0, half, pack, (jnp.zeros((1, 1), jnp.int32), jnp.zeros((8, raised), f32))
        )
        digits = digits.astype(jnp.int32)
        bundle[...] = packed[...].astype(bf16)
        bundle_to[...] = jnp.where(digits[2:3] > 0, digits[0:1] * 256 + digits[1:2], slot_count)
        for copy in bundle_copies():
            copy.start()

    table_load.wait()
    back_rows[0, :, :n] = table[3 * n : 4 * n, :]
    back_rows[0, :, n:] = -table[4 * n : 5 * n, :]
    back_rows[1, :, :n] = table[4 * n : 5 * n, :]
    back_rows[1, :, n:] = table[3 * n : 4 * n, :]
    block = 64

    def multipliers(t, carry):
        start = pl.multiple_of(t * block, block)
        row = lax.broadcasted_iota(jnp.int32, (block, h + 128), 0) + start
        col = lax.broadcasted_iota(jnp.int32, (block, h + 128), 1)
        along = (row - jnp.where(row >= h, n, 0)).astype(f32) * (2.0 / n)
        across = jnp.where(col < h, col, -h).astype(f32) * (2.0 / n)
        power = across * across + along * along
        scale = (1.0 / (n * n)) / jnp.where(power > 0, power, 1.0)
        scale = jnp.where(col <= h, scale, 0.0)
        weights[0, pl.ds(start, block), :] = (along * along - 3.0 * across * across) * along * scale
        weights[1, pl.ds(start, block), :] = (across * across - 3.0 * along * along) * across * scale
        return carry

    lax.fori_loop(0, n // block, multipliers, 0)

    def two(b, a, c):
        place(
            jnp.concatenate([got_tiles[b, a], got_tiles[b, c]], axis=0),
            jnp.concatenate([got_aux[b, a], got_aux[b, c]], axis=1),
        )

    def receive(u, carry):
        first, second = place_of(2 * u), place_of(2 * u + 1)
        for copy in copies(0, first):
            copy.wait_recv()

        @pl.when(second > 0)
        def _():
            for copy in copies(0, second):
                copy.wait_recv()

        @pl.when(second == 0)
        def _():
            got_tiles[0, 0] = tiles[0, 0]
            got_aux[0, 0] = aux[0, 0]

        two(0, first, second)

        @pl.when(jnp.logical_and(has_down, 2 * u >= half))
        def _():
            for t in (2 * u, 2 * u + 1):
                for copy in copies(1, t):
                    copy.wait_recv()
            two(1, 2 * u, 2 * u + 1)

        return carry

    lax.fori_loop(0, half, receive, 0)

    @pl.when(has_down)
    def _():
        for copy in bundle_copies():
            copy.wait_recv()
        place(far[...], far_to[...])

    image[...] = patch[...].astype(bf16)

    width = tile
    has = [has_up, has_down, j > 0, j < n_py - 1]
    beside = [(i - 1, j), (i + 1, j), (i, j - 1), (i, j + 1)]
    ends = [pl.ds(0, width), pl.ds(n - width, width)]
    inner = pl.ds(width, n - 2 * width)
    pairs = [pl.ds(0, 2), pl.ds(2, 2)]

    def row_copy(side, pair):
        return pltpu.make_async_remote_copy(
            src_ref=fields.at[pairs[pair], ends[side], :],
            dst_ref=from_rows.at[1 - side, pairs[pair]],
            send_sem=send_v.at[side, pair],
            recv_sem=recv_v.at[1 - side, pair],
            device_id=beside[side],
            device_id_type=MESH,
        )

    def col_copy(side, piece):
        if piece < 2:
            part, span = pl.ds(0, 4), ends[piece]
            source = corners.at[side, :, span, :]
        else:
            part, span = pairs[piece - 2], inner
            source = fields.at[part, inner, ends[side]]
        return pltpu.make_async_remote_copy(
            src_ref=source,
            dst_ref=from_cols.at[1 - side, part, span, :],
            send_sem=send_h.at[side, piece],
            recv_sem=recv_h.at[1 - side, piece],
            device_id=beside[2 + side],
            device_id_type=MESH,
        )

    def send_strips(pair):
        for side in range(2):

            @pl.when(has[side])
            def _():
                row_copy(side, pair).start()

            @pl.when(has[2 + side])
            def _():
                col_copy(side, 2 + pair).start()

    pixels = image[...].astype(f32)
    row_sign = 1.0 - 2.0 * (lax.broadcasted_iota(jnp.int32, (n, 1), 0) % 2).astype(f32)
    col_sign = 1.0 - 2.0 * (lax.broadcasted_iota(jnp.int32, (1, n), 1) % 2).astype(f32)
    row_edge = jnp.sum(pixels * row_sign, axis=0, keepdims=True) * (1.0 / n)

    def write_real(start, value):
        sign = 1.0 - 2.0 * (lax.broadcasted_iota(jnp.int32, (value.shape[0], 1), 0) % 2).astype(f32)
        fields[0, pl.ds(start, value.shape[0]), :] = (value + sign * row_edge).astype(bf16)

    def write_imag(start, value):
        own = image[pl.ds(start, value.shape[0]), :].astype(f32)
        col_edge = jnp.sum(own * col_sign, axis=1, keepdims=True) * (1.0 / n)
        fields[1, pl.ds(start, value.shape[0]), :] = (-value - col_edge * col_sign).astype(bf16)

    blocked_dot(n, image, slope, write_real)
    blocked_dot(n, slope, image, write_imag)
    send_strips(0)

    def write_halves(start, value):
        halves[pl.ds(start, value.shape[0]), :] = value.astype(bf16)

    def write_spectrum(start, value):
        spectrum[pl.ds(start, value.shape[0]), :] = value

    blocked_dot(n, image, forward, write_halves)
    blocked_dot(2 * n, down, halves, write_spectrum)

    first = lax.broadcasted_iota(jnp.int32, (1, h), 1) == 0

    def multiply(t, carry):
        start = pl.multiple_of(t * block, block)
        low = pl.ds(start, block)
        high = pl.ds(pl.multiple_of(start + n, block), block)
        z_r = spectrum[low, :h] - jnp.where(first, 0.0, spectrum[high, h:])
        z_i = -(spectrum[high, :h] + jnp.where(first, 0.0, spectrum[low, h:]))
        e_r = spectrum[low, h : h + 128]
        e_i = -spectrum[high, h : h + 128]
        k_r, k_i = weights[0, low, :h], weights[1, low, :h]
        q_r, q_i = weights[0, low, h:], weights[1, low, h:]
        last = lax.broadcasted_iota(jnp.int32, (block, 1), 0) + start == h
        r_last, r_rest = jnp.where(last, k_r, 0.0), jnp.where(last, 0.0, k_r)
        q_last, q_rest = jnp.where(last, q_r, 0.0), jnp.where(last, 0.0, q_r)
        parts = (
            (r_last * z_r - k_i * z_i, r_last * z_i + k_i * z_r, q_last * e_r, q_last * e_i),
            (r_rest * z_i, -r_rest * z_r, q_i * e_r + q_rest * e_i, q_i * e_i - q_rest * e_r),
        )
        for s, (g_r, g_i, top_r, top_i) in enumerate(parts):
            spectra[low, s * h : s * h + 128] = (g_r[:, :128] - top_i).astype(bf16)
            spectra[low, s * h + 128 : (s + 1) * h] = g_r[:, 128:].astype(bf16)
            spectra[high, s * h : s * h + 128] = (g_i[:, :128] + top_r).astype(bf16)
            spectra[high, s * h + 128 : (s + 1) * h] = g_i[:, 128:].astype(bf16)
        return carry

    lax.fori_loop(0, n // block, multiply, 0)

    for part in range(2):

        def write_columns(start, value, part=part):
            rows = pl.ds(start, value.shape[0])
            for s in range(2):
                columns[s, rows, part * h : (part + 1) * h] = value[:, s * h : (s + 1) * h].astype(bf16)

        blocked_dot(n, back_rows.at[part], spectra, write_columns)
    for s in range(2):

        def write_three(start, value, s=s):
            fields[2 + s, pl.ds(start, value.shape[0]), :] = value.astype(bf16)

        blocked_dot(n, columns.at[s], back_cols, write_three)
    send_strips(1)

    out[:, inner, :] = fields[:, inner, :]

    def ramps(shape, dim):
        steps = lax.broadcasted_iota(jnp.int32, shape, dim).astype(f32)
        return (steps + 0.5) * (1.0 / width), (width - 0.5 - steps) * (1.0 / width)

    for side, ramp in enumerate(ramps((1, width, 1), 1)):
        span = ends[side]

        @pl.when(has[side])
        def _():
            for pair in range(2):
                row_copy(1 - side, pair).wait_recv()
            own, other = fields[:, span, :].astype(f32), from_rows[side].astype(f32)
            out[:, span, :] = (ramp * own + (1.0 - ramp) * other).astype(bf16)

        @pl.when(jnp.logical_not(has[side]))
        def _():
            out[:, span, :] = fields[:, span, :]

        for other in range(2):
            corners[other, :, span, :] = out[:, span, ends[other]]

            @pl.when(has[2 + other])
            def _():
                col_copy(other, side).start()

    for piece in (2, 3, 0, 1):
        part, span = (pl.ds(0, 4), ends[piece]) if piece < 2 else (pairs[piece - 2], inner)
        for side, ramp in enumerate(ramps((1, 1, width), 2)):

            @pl.when(has[2 + side])
            def _():
                col_copy(1 - side, piece).wait_recv()
                own = out[part, span, ends[side]].astype(f32)
                other = from_cols[side, part, span, :].astype(f32)
                out[part, span, ends[side]] = (ramp * own + (1.0 - ramp) * other).astype(bf16)

    for side in range(2):

        @pl.when(has[side])
        def _():
            for pair in range(2):
                row_copy(side, pair).wait_send()

        @pl.when(has[2 + side])
        def _():
            for piece in range(4):
                col_copy(side, piece).wait_send()

    def finish(t, carry):
        o = place_of(t)

        @pl.when(o > 0)
        def _():
            for copy in copies(0, o):
                copy.wait_send()

        @pl.when(has_up)
        def _():
            for copy in copies(1, o):
                copy.wait_send()

        return carry

    lax.fori_loop(0, n_py, finish, 0)

    @pl.when(has_down)
    def _():
        for copy in bundle_copies():
            copy.wait_send()


def widen_kernel(narrow, out, held, wide, arrive, leave):
    pieces = [(k, pl.ds(r, PATCH // 2)) for k in range(held.shape[0]) for r in (0, PATCH // 2)]
    loads = [
        pltpu.make_async_copy(narrow.at[k, rows], held.at[k, rows], arrive.at[t])
        for t, (k, rows) in enumerate(pieces)
    ]
    stores = [
        pltpu.make_async_copy(wide.at[k, rows], out.at[k, rows], leave.at[t])
        for t, (k, rows) in enumerate(pieces)
    ]
    for copy in loads:
        copy.start()
    for load, store, (k, rows) in zip(loads, stores, pieces):
        load.wait()
        wide[k, rows] = held[k, rows].astype(jnp.float32)
        store.start()
    for copy in stores:
        copy.wait()


def on_device(kappa, send_list, dest_slot, send_count):
    n_px = lax.axis_size("px")
    n_py = lax.axis_size("py")
    cap = send_list.shape[2]
    tile = kappa.shape[1]
    n = PATCH
    raised = RAISED * n // tile
    anywhere = pl.BlockSpec(memory_space=pl.ANY)
    vmem, bf16, f32 = pltpu.VMEM, jnp.bfloat16, jnp.float32
    dma = pltpu.SemaphoreType.DMA
    tiles, aux = (2, n_py, cap, tile), (2, n_py, 1, cap)
    blended = pl.pallas_call(
        functools.partial(flexion_kernel, n_px, n_py),
        out_shape=jax.ShapeDtypeStruct((4, n, n), bf16),
        in_specs=[anywhere] * 5,
        out_specs=pl.BlockSpec(memory_space=vmem),
        scratch_shapes=[
            vmem((5 * n, n), bf16),
            vmem((2, n, 2 * n), bf16),
            vmem((2, n, n // 2 + 128), f32),
            vmem(kappa.shape, bf16),
            vmem(kappa.shape, f32),
            vmem((cap, tile), f32),
            vmem(tiles, bf16),
            vmem(aux, jnp.int32),
            vmem(tiles, bf16),
            vmem(aux, jnp.int32),
            pltpu.SMEM((2, n_py, cap), jnp.int32),
            vmem((2, n_py, cap), jnp.int32),
            pltpu.SMEM(send_count.shape, jnp.int32),
            vmem((raised, tile), f32),
            vmem((raised, tile), bf16),
            vmem((1, raised), jnp.int32),
            vmem((raised, tile), bf16),
            vmem((1, raised), jnp.int32),
            vmem((n, n), f32),
            vmem((n, n), bf16),
            vmem((n, n), bf16),
            vmem((2 * n, n), f32),
            vmem((2 * n, n), bf16),
            vmem((2, n, n), bf16),
            vmem((4, n, n), bf16),
            vmem((2, 4, tile, n), bf16),
            vmem((2, 4, n, tile), bf16),
            vmem((2, 4, n, tile), bf16),
            dma((7,)),
        ]
        + [dma((2, n_py))] * 4
        + [dma((2, 2))] * 2
        + [dma((2, 4))] * 2
        + [dma((2,))] * 2,
        compiler_params=pltpu.CompilerParams(
            collective_id=0, has_side_effects=True, vmem_limit_bytes=58 * 2**20
        ),
        name="flexion",
    )(kappa, send_list, dest_slot, send_count, transform_tables(n))
    return pl.pallas_call(
        widen_kernel,
        out_shape=jax.ShapeDtypeStruct((4, n, n), f32),
        in_specs=[anywhere],
        out_specs=anywhere,
        scratch_shapes=[vmem((4, n, n), bf16), vmem((4, n, n), f32), dma((8,)), dma((8,))],
        compiler_params=pltpu.CompilerParams(vmem_limit_bytes=58 * 2**20),
        name="widen",
    )(blended)


def solution(mesh):
    placed = (
        P(("px", "py"), None),
        P(("px", "py"), None, None),
        P(("px", "py"), None, None),
        P(("px", "py"), None),
    )
    return jax.shard_map(
        on_device, mesh=mesh, in_specs=placed, out_specs=P(None, "px", "py"), check_vma=False
    )
```
